256 devices in a mesh: trc: 4 (over y), lat: 4 (over x_lo, core), lon: 16 (over x_hi, z).
Axes of the slice: x: 4 (x_hi: 2, x_lo: 2; x = x_hi * 2 + x_lo), y: 4, z: 8, core: 2. Of those that a mesh axis runs over, the one named last changes fastest.
Arguments:
- species_concentrations: float32 [32, 8, 128, 2048], P('trc', None, 'lat', 'lon'), may hold values from 0.2 to 4
- zonal_velocity_array: float32 [8, 128, 2048], P('trc', 'lat', 'lon'), may hold values from -2.5 to 2.5
- meridional_velocity_array: float32 [8, 128, 2048], P('trc', 'lat', 'lon'), may hold values from -2.5 to 2.5
- thermal_anomaly: float32 [8, 128, 2048], P('trc', 'lat', 'lon'), may hold values from -6 to 6
- ocean_top_height_grid: float32 [128, 2048], P('lat', 'lon'), may hold values from -6 to 6
- water_layer_tally: int32 [128, 2048], P('lat', 'lon'), may hold values from 0 to 8
- species_interaction_table: float32 [32, 32], replicated, may hold values from -1 to 1
- species_production_pace: float32 [32], replicated, may hold values from 0.2 to 2
- photon_uptake: float32 [32], replicated, may hold values from 0.01 to 0.1
Outputs:
- updated_tracers: float32 [32, 8, 128, 2048], P('trc', None, 'lat', 'lon')
- east_out: float32 [8, 128, 2048], P('trc', 'lat', 'lon')
- north_out: float32 [8, 128, 2048], P('trc', 'lat', 'lon')
- temperature_out: float32 [8, 128, 2048], P('trc', 'lat', 'lon')
- height_out: float32 [128, 2048], P('lat', 'lon')
The draws below stay inside these ranges and needn't reach their ends.
Inputs may be any that keep to these rules, and one draw needn't show every extreme that they name: `water_layer_tally`: the number of wet levels of a column, counted from the surface; cells below it, and whole columns with 0, are land.
All inputs are finite; a program needn't handle non-finite values.
Results may differ from the reference program's by a relative error of at most 0.0003.
Values sent between devices are 32-bit elements; how exact they have to be, the bound alone decides.
A program may use at most 64 MiB of HBM per device.

```python
import math
import jax
import jax.numpy as jnp
from jax import lax

TRACERS = 32
VERTICAL_LAYERS = 8
MERIDIAN_STRIPS = 128
ZONAL_STRIPS = 2048


def set_ends(array, key, smallest, largest):
    extent = array.shape
    place = [jax.random.randint(jax.random.fold_in(key, axis), (), 0, extent[axis]) for axis in range(len(extent))]
    array = array.at[tuple(place)].set(smallest)
    longest = extent.index(max(extent))
    place[longest] = (place[longest] + 1) % extent[longest]
    return array.at[tuple(place)].set(largest)


def shard_levels(rng, extent, pieces, smallest, top_value):
    level, own = 1.0, jax.random.fold_in(rng, 6)
    for position, parts in pieces:
        draws = jnp.exp(jax.random.uniform(jax.random.fold_in(own, position), (parts,), jnp.float32, smallest / len(pieces), top_value / len(pieces)))
        level = level * jnp.repeat(draws, extent[position] // parts).reshape([-1 if axis == position else 1 for axis in range(len(extent))])
    return level


def bell_draw(rng, dims, scale, limit, shards=(), kind=jnp.bfloat16):
    result = scale * jax.random.normal(rng, dims, jnp.float32)
    if shards:
        result = result * shard_levels(rng, dims, shards, -0.22, 0.18)
    return jnp.clip(result, -limit, limit).astype(kind)


def setup_inputs(seed: int = 0) -> dict:
    splits = jax.random.split(jax.random.key(seed), 10)
    return {
        "species_concentrations": jnp.clip(jnp.exp(math.log(4.0) - 2.9957323 * jax.random.uniform(splits[0], (TRACERS, VERTICAL_LAYERS, MERIDIAN_STRIPS, ZONAL_STRIPS), jnp.float32) ** shard_levels(splits[0], (TRACERS, VERTICAL_LAYERS, MERIDIAN_STRIPS, ZONAL_STRIPS), ((0, 4), (2, 4), (3, 16)), -0.2, 0.2)), 0.2, 4.0),
        "zonal_velocity_array": bell_draw(splits[1], (VERTICAL_LAYERS, MERIDIAN_STRIPS, ZONAL_STRIPS), 0.16, 2.5, ((0, 4), (1, 4), (2, 16)), jnp.float32),
        "meridional_velocity_array": bell_draw(splits[2], (VERTICAL_LAYERS, MERIDIAN_STRIPS, ZONAL_STRIPS), 0.16, 2.5, ((0, 4), (1, 4), (2, 16)), jnp.float32),
        "thermal_anomaly": bell_draw(splits[3], (VERTICAL_LAYERS, MERIDIAN_STRIPS, ZONAL_STRIPS), 1.0, 6.0, ((0, 4), (1, 4), (2, 16)), jnp.float32),
        "ocean_top_height_grid": bell_draw(splits[4], (MERIDIAN_STRIPS, ZONAL_STRIPS), 0.5, 6.0, ((0, 4), (1, 16)), jnp.float32),
        "water_layer_tally": set_ends(jax.random.randint(splits[5], (MERIDIAN_STRIPS, ZONAL_STRIPS), 0, VERTICAL_LAYERS + 1), jax.random.fold_in(splits[5], 1), 0, VERTICAL_LAYERS).astype(jnp.int32),
        "species_interaction_table": bell_draw(splits[6], (TRACERS, TRACERS), TRACERS ** -0.5, 1.0, (), jnp.float32),
        "species_production_pace": jnp.clip(jnp.exp(jax.random.uniform(splits[7], (TRACERS,), jnp.float32, math.log(0.2), math.log(2.0))), 0.2, 2.0),
        "photon_uptake": jnp.clip(jnp.exp(jax.random.uniform(splits[8], (TRACERS,), jnp.float32, math.log(0.01), math.log(0.1))), 0.01, 0.1),
    }


HIGHEST = lax.Precision.HIGHEST
TIME_STEP = 0.1
GRAVITY = 1.0
VISCOSITY = 0.2
BOTTOM_DRAG = 0.05
DEPTH_SCALE = 0.5
CORIOLIS_SCALE = 0.5
COLUMN_DEPTH = 2.0
WATER_ABSORB = 0.2
HALF_LIGHT = 0.5
REACT_STEP = 0.1
WARMING_WEIGHT = 1.0


def limited_slope(ahead, behind):
    smaller = jnp.minimum(jnp.abs(ahead), jnp.abs(behind))
    return jnp.where(ahead * behind > 0, jnp.where(ahead > 0, smaller, -smaller), jnp.zeros_like(smaller))


def face_flux(before, center, after, beyond, vel_here, vel_next, wet_here, wet_next):
    courant = 0.5 * (vel_here + vel_next) * wet_here * wet_next
    upwind_pos = center + 0.5 * (1.0 - courant) * limited_slope(after - center, center - before)
    upwind_neg = after - 0.5 * (1.0 + courant) * limited_slope(beyond - after, after - center)
    return courant * jnp.where(courant >= 0, upwind_pos, upwind_neg)


def transport(field, flow_east, flow_north, wet):
    free_top_height, width = field.shape[-2], field.shape[-1]
    rows = slice(2, free_top_height - 2)
    cols = slice(2, width - 2)
    flux_x = face_flux(field[..., rows, 0:width - 3], field[..., rows, 1:width - 2], field[..., rows, 2:width - 1], field[..., rows, 3:width],
                       flow_east[..., rows, 1:width - 2], flow_east[..., rows, 2:width - 1], wet[..., rows, 1:width - 2], wet[..., rows, 2:width - 1])
    flux_y = face_flux(field[..., 0:free_top_height - 3, cols], field[..., 1:free_top_height - 2, cols], field[..., 2:free_top_height - 1, cols], field[..., 3:free_top_height, cols],
                       flow_north[..., 1:free_top_height - 2, cols], flow_north[..., 2:free_top_height - 1, cols], wet[..., 1:free_top_height - 2, cols], wet[..., 2:free_top_height - 1, cols])
    return field[..., rows, cols] - (flux_x[..., 1:] - flux_x[..., :-1]) - (flux_y[..., 1:, :] - flux_y[..., :-1, :])


def periodic_pad(field, width):
    field = jnp.concatenate([field[..., -width:], field, field[..., :width]], -1)
    pads = [(0, 0)] * (field.ndim - 2) + [(width, width), (0, 0)]
    return jnp.pad(field, pads)


def lat_next(field):
    return jnp.concatenate([field[..., 1:, :], jnp.zeros_like(field[..., :1, :])], -2)


def lat_prev(field):
    return jnp.concatenate([jnp.zeros_like(field[..., :1, :]), field[..., :-1, :]], -2)


def ocean_core(stacked, north, south, east, west, wet, coriolis):
    count = (stacked.shape[0] - 1) // 2
    zonal_flow_value = stacked[:count]
    meridional_flow_value = stacked[count:2 * count]
    free_top_height = stacked[2 * count]
    lap_east = north[:count] + south[:count] + east[:count] + west[:count] - 4.0 * zonal_flow_value
    lap_north = north[count:2 * count] + south[count:2 * count] + east[count:2 * count] + west[count:2 * count] - 4.0 * meridional_flow_value
    grad_x = 0.5 * (east[2 * count] - west[2 * count])
    grad_y = 0.5 * (north[2 * count] - south[2 * count])
    div_levels = 0.5 * (east[:count] - west[:count]) + 0.5 * (north[count:2 * count] - south[count:2 * count])
    new_east = wet * (zonal_flow_value + TIME_STEP * (coriolis * meridional_flow_value - GRAVITY * grad_x + VISCOSITY * lap_east - BOTTOM_DRAG * zonal_flow_value))
    new_north = wet * (meridional_flow_value + TIME_STEP * (-coriolis * zonal_flow_value - GRAVITY * grad_y + VISCOSITY * lap_north - BOTTOM_DRAG * meridional_flow_value))
    return new_east, new_north, free_top_height, jnp.sum(div_levels, 0)


def light_profile(absorbed, wet, surface):
    levels = absorbed.shape[0]
    layer = (COLUMN_DEPTH / levels) * (WATER_ABSORB + absorbed) * wet
    above = jnp.cumsum(layer, 0) - layer
    top_light = surface[None, :, None] * jnp.exp(-above)
    return top_light * (1.0 - jnp.exp(-layer)), top_light / (top_light + HALF_LIGHT)


def reference(species_concentrations, zonal_velocity_array, meridional_velocity_array, thermal_anomaly, ocean_top_height_grid, water_layer_tally, species_interaction_table, species_production_pace, photon_uptake):
    depth_index = jnp.arange(VERTICAL_LAYERS).astype(jnp.int32)
    wet = (depth_index[:, None, None] < water_layer_tally[None]).astype(jnp.float32)
    lat_index = jnp.arange(MERIDIAN_STRIPS).astype(jnp.float32)
    angle = math.pi * ((lat_index + 0.5) / MERIDIAN_STRIPS - 0.5)
    coriolis = CORIOLIS_SCALE * jnp.sin(angle)[:, None]
    surface = 1.0 + jnp.cos(angle)
    east_start = wet * zonal_velocity_array
    north_start = wet * meridional_velocity_array
    zonal_flow_value, meridional_flow_value, free_top_height = east_start, north_start, ocean_top_height_grid
    for substep in range(2):
        stacked = jnp.concatenate([zonal_flow_value, meridional_flow_value, free_top_height[None]], 0)
        zonal_flow_value, meridional_flow_value, free_top_height, divergence = ocean_core(stacked, lat_next(stacked), lat_prev(stacked),
                                                             jnp.roll(stacked, -1, -1), jnp.roll(stacked, 1, -1), wet, coriolis)
        free_top_height = free_top_height - TIME_STEP * DEPTH_SCALE * divergence
    flow_east = periodic_pad(east_start, 2)
    flow_north = periodic_pad(north_start, 2)
    wet_pad = periodic_pad(wet, 2)

    def move_one(field):
        for substep in range(2):
            field = transport(periodic_pad(field, 2), flow_east, flow_north, wet_pad)
        return field

    moved = lax.map(move_one, species_concentrations)
    absorbed = jnp.einsum("n,nkyx->kyx", photon_uptake, jnp.abs(moved), precision=HIGHEST)
    solar_warming, light_factor = light_profile(absorbed, wet, surface)
    mixed = jnp.einsum("mn,nkyx->mkyx", species_interaction_table, moved, precision=HIGHEST)
    species_postchemistry = moved + wet * REACT_STEP * (mixed + species_production_pace[:, None, None, None] * light_factor * moved)
    return species_postchemistry, zonal_flow_value, meridional_flow_value, thermal_anomaly + WARMING_WEIGHT * solar_warming, free_top_height
```

```python
import functools
import math

import jax
import jax.numpy as jnp
from jax import lax
from jax.experimental import pallas as pl
from jax.experimental.pallas import tpu as pltpu
from jax.sharding import PartitionSpec as P

MESH = pl.DeviceIdType.MESH
F32 = jnp.float32
DT = 0.1
CHUNKS = ((0, 12), (12, 20))
HALO = 4
UNROLL = 4


def in_pieces(rows):
    pieces = [(0, HALO), (rows - HALO, HALO)]
    need, done = [], HALO
    for first, count in CHUNKS:
        end = min(first + count + HALO, rows - HALO)
        if end > done:
            pieces.append((done, end - done))
            done = end
        need.append(len(pieces))
    return pieces, need


def minmod(x, y):
    return jnp.maximum(jnp.minimum(x, y), jnp.minimum(jnp.maximum(x, y), 0.0))


def lanes(x, shift):
    shift = shift % x.shape[-1]
    return pltpu.roll(x, shift, x.ndim - 1) if shift else x


def rows_by(x, shift):
    shift = -shift % x.shape[0]
    return pltpu.roll(x, shift, 0) if shift else x


def kernel(
    x, u_in, v_in, th_in, h_in, w_in, table, pace, uptake,
    o_x, o_u, o_v, o_t, o_h,
    tx, c0, c1, c2, out, ry, pk_own, pk_got, cc, cf,
    vs, mom, dp, dp_got, h1, ab, s_own, s_got, fl, w01, prod,
    in_s, in_r, lon_s, lon_r, lat_s, lat_r, vs_s, vs_r, dp_s, dp_r, h_s, h_r,
    s_s, s_r, out_s, out_r, loc,
):
    rows, width = h_in.shape
    n_lat, n_lon = lax.axis_size("lat"), lax.axis_size("lon")
    t, la, lo = lax.axis_index("trc"), lax.axis_index("lat"), lax.axis_index("lon")
    other = [lax.rem(t + d, 4) for d in (1, 2, 3)]
    source = [lax.rem(t + 4 - d, 4) for d in (1, 2, 3)]
    east, west = lax.rem(lo + 1, n_lon), lax.rem(lo + n_lon - 1, n_lon)
    north, south = lax.rem(la + 1, n_lat), lax.rem(la + n_lat - 1, n_lat)
    pieces, need = in_pieces(rows)

    def remote(src, dst, send, recv, where):
        return pltpu.make_async_remote_copy(
            src_ref=src, dst_ref=dst, send_sem=send, recv_sem=recv, device_id=where, device_id_type=MESH
        )

    sends = []

    def go(copy):
        copy.start()
        sends.append(copy)
        return copy

    barrier = pltpu.get_barrier_semaphore()
    friends = [{"trc": g} for g in other] + [{"lon": east}, {"lon": west}, {"lat": north}, {"lat": south}]
    for friend in friends:
        pl.semaphore_signal(barrier, inc=1, device_id=friend, device_id_type=MESH)

    depth = w_in[...].astype(F32)

    def wet_of(level, depths):
        return jnp.where(level < depths, 1.0, 0.0)

    own = pl.ds(8, rows)
    for kk in range(2):
        wet = wet_of((2 * t + kk).astype(F32), depth)
        vs[1, kk, own] = wet * u_in[kk]
        vs[1, 2 + kk, own] = wet * v_in[kk]
    vs[1, 4, own] = h_in[...]
    vs[1, 5, own] = depth

    def turn(target, dst, base):
        for kk in range(2):
            for n in range(8):
                dst[kk, pl.ds(base + n, rows, stride=8), :] = x[n, 2 * target + kk]

    pl.semaphore_wait(barrier, len(friends))
    vs_lon = [
        go(remote(vs.at[1, :, own], vs.at[0, :, own], vs_s.at[0], vs_r.at[0], {"lon": east})),
        go(remote(vs.at[1, :, own], vs.at[2, :, own], vs_s.at[1], vs_r.at[1], {"lon": west})),
    ]
    incoming = {}

    def send_piece(d, p):
        first, count = pieces[p]
        incoming[d, p] = go(
            remote(
                tx.at[d, :, pl.ds(8 * first, 8 * count)],
                c0.at[t, :, pl.ds(8 * (first + HALO), 8 * count)],
                in_s.at[d, p], in_r.at[d, p], {"trc": other[d]},
            )
        )

    for d in (1, 0, 2):
        turn(other[d], tx.at[d], 0)
        send_piece(d, 0)
        send_piece(d, 1)
    turn(t, c0.at[t], 8 * HALO)
    for p in range(2, len(pieces)):
        for d in (1, 0, 2):
            send_piece(d, p)

    for copy in vs_lon:
        copy.wait_recv()
    top, low = pl.ds(rows, 8), pl.ds(8, 8)
    vs_lat = [
        go(remote(vs.at[:, :, top], vs.at[:, :, pl.ds(0, 8)], vs_s.at[2], vs_r.at[2], {"lat": north})),
        go(remote(vs.at[:, :, low], vs.at[:, :, pl.ds(rows + 8, 8)], vs_s.at[3], vs_r.at[3], {"lat": south})),
    ]

    lane = lax.broadcasted_iota(jnp.int32, (8, width), 1)
    slot = lane // 8
    lane32 = lane % 32

    def tile(buf, g, kk, r):
        return buf[g, kk, pl.ds(pl.multiple_of(8 * (r + HALO), 8), 8), :]

    def pack(q):
        pos = (q + 1) % (rows // 4)
        for kk in range(2):
            to_west = to_east = jnp.zeros((8, width), F32)
            for j in range(4):
                for g in range(4):
                    s = 4 * g + j
                    turned = lanes(tile(c0, g, kk, 4 * q + j), 8 * (s + 1))
                    to_west = jnp.where(slot == (s + 1) % 16, turned, to_west)
                    to_east = jnp.where(slot == s, turned, to_east)
            pk_own[0, kk, pos] = to_west
            pk_own[1, kk, pos] = to_east

    def send_pack(i, quads):
        pos = [(q + 1) % (rows // 4) for q in quads]
        part = pl.ds(min(pos), len(pos))
        return [
            go(remote(pk_own.at[1, :, part], pk_got.at[1, :, part], lon_s.at[0, i], lon_r.at[0, i], {"lon": east})),
            go(remote(pk_own.at[0, :, part], pk_got.at[0, :, part], lon_s.at[1, i], lon_r.at[1, i], {"lon": west})),
        ]

    def strips(q):
        pos = (q + 1) % (rows // 4)
        for kk in range(2):
            from_west, from_east = pk_got[1, kk, pos], pk_got[0, kk, pos]
            own_w, own_e = pk_own[0, kk, pos], pk_own[1, kk, pos]
            for j in range(4):
                left = lanes(jnp.where(slot % 4 == j, from_west, own_w), -8 * j)
                right = lanes(jnp.where(slot % 4 == j, own_e, from_east), 16 - 8 * j)
                c0[4, kk, pl.ds(8 * (4 * q + j + HALO), 8), :] = jnp.where(lane32 < 16, left, right)

    for p in (0, 1):
        for d in range(3):
            incoming[d, p].wait_recv()
    last = rows // 4 - 1
    pack(last)
    pack(0)
    pk = send_pack(0, (last, 0))

    for copy in vs_lat:
        copy.wait_recv()

    @pl.when(la == 0)
    def _():
        for b in range(3):
            for f in range(6):
                vs[b, f, 0:8] = jnp.zeros((8, width), F32)

    @pl.when(la == n_lat - 1)
    def _():
        for b in range(3):
            for f in range(6):
                vs[b, f, rows + 8 : rows + 16] = jnp.zeros((8, width), F32)

    vlane = lax.broadcasted_iota(jnp.int32, (rows + 16, width), 1) % 32

    def strip_form(f):
        w_, o_, e_ = vs[0, f], vs[1, f], vs[2, f]
        left = jnp.where(vlane < 8, lanes(w_, 8), lanes(o_, 8))
        right = jnp.where(vlane < 24, lanes(o_, 24), lanes(e_, 24))
        first = jnp.where(vlane < 16, left, right)
        lane_ = lax.broadcasted_iota(jnp.int32, first.shape, 1)
        first = jnp.where(lane_ < 32, first, 0.0)
        first = first + lanes(first, 32)
        return first + lanes(first, 64)

    def weights(a):
        ap, an = jnp.maximum(a, 0.0), jnp.minimum(a, 0.0)
        return ap, 0.5 * ap * (1.0 - ap), an, -0.5 * an * (1.0 + an)

    for form in range(2):
        get = (lambda f: vs[1, f]) if form == 0 else strip_form
        dep = get(5)
        for kk in range(2):
            wet = wet_of((2 * t + kk).astype(F32), dep)
            u, v = get(kk), get(2 + kk)
            ax = 0.5 * (u + lanes(u, -1)) * wet * lanes(wet, -1)
            ap, bp, an, bn = weights(ax)
            cc[form, 0, kk], cc[form, 1, kk] = ap, bp
            cc[form, 2, kk], cc[form, 3, kk] = lanes(an, 1), lanes(bn, 1)
            ay = 0.5 * (v + rows_by(v, 1)) * wet * rows_by(wet, 1)
            for i, w in enumerate(weights(ay)):
                cc[form, 4 + i, kk] = w

    @pl.loop(1, rows + 2 * HALO)
    def _(r):
        for form in range(2):
            for i in range(8):
                for kk in range(2):
                    cf[form, i, kk, r] = jnp.broadcast_to(cc[form, i, kk, pl.ds(r + 8 - HALO, 1), :], (8, width))

    big = rows + 16
    row_no = (la * rows - 8 + lax.broadcasted_iota(jnp.int32, (big, 1), 0)).astype(F32)
    angle = math.pi * ((row_no + 0.5) / (rows * n_lat) - 0.5)
    coriolis = 0.5 * jnp.sin(angle)
    surface = 1.0 + jnp.cos(angle)
    wide = lambda ref, f: jnp.concatenate([ref[0, f], ref[1, f], ref[2, f]], axis=1)

    def momentum(u, v, h, wet):
        h_x = 0.5 * (lanes(h, -1) - lanes(h, 1))
        h_y = 0.5 * (rows_by(h, 1) - rows_by(h, -1))
        lap_u = rows_by(u, 1) + rows_by(u, -1) + lanes(u, -1) + lanes(u, 1) - 4.0 * u
        lap_v = rows_by(v, 1) + rows_by(v, -1) + lanes(v, -1) + lanes(v, 1) - 4.0 * v
        new_u = wet * (u + DT * (coriolis * v - h_x + 0.2 * lap_u - 0.05 * u))
        new_v = wet * (v + DT * (-coriolis * u - h_y + 0.2 * lap_v - 0.05 * v))
        return new_u, new_v

    def divergence(u, v):
        d = 0.5 * (lanes(u, -1) - lanes(u, 1)) + 0.5 * (rows_by(v, 1) - rows_by(v, -1))
        return d[8 : 8 + rows, width : 2 * width]

    def dp_stage(i):
        partner = t + 1 - 2 * lax.rem(t, 2) if i % 2 == 0 else 3 - t
        return go(remote(dp.at[i], dp_got.at[i], dp_s.at[i], dp_r.at[i], {"trc": partner}))

    wide_depth = wide(vs, 5)
    wide_h = wide(vs, 4)
    div = jnp.zeros((rows, width), F32)
    for kk in range(2):
        u, v = wide(vs, kk), wide(vs, 2 + kk)
        div = div + divergence(u, v)
        mom[kk], mom[2 + kk] = momentum(u, v, wide_h, wet_of((2 * t + kk).astype(F32), wide_depth))
    dp[0] = div
    stage = dp_stage(0)

    for copy in pk:
        copy.wait_recv()
    strips(last)
    strips(0)
    lat = [
        go(remote(c0.at[:, :, pl.ds(8 * rows, 8 * HALO)], c0.at[:, :, pl.ds(0, 8 * HALO)],
                  lat_s.at[0], lat_r.at[0], {"lat": north})),
        go(remote(c0.at[:, :, pl.ds(8 * HALO, 8 * HALO)], c0.at[:, :, pl.ds(8 * (rows + HALO), 8 * HALO)],
                  lat_s.at[1], lat_r.at[1], {"lat": south})),
    ]
    stage.wait_recv()
    dp[1] = dp[0] + dp_got[0]
    stage = dp_stage(1)

    sub = lax.broadcasted_iota(jnp.int32, (8, width), 0)

    def column(ref, g):
        col = jnp.full((8, width), ref[8 * g], F32)
        for n in range(1, 8):
            col = jnp.where(sub == n, ref[8 * g + n], col)
        return col

    uptakes = [column(uptake, g) for g in range(4)]
    for g in range(4):
        prod[g] = column(pace, g)

    def step(src, dst, first, count, finish):
        for kk in range(2):
            def coef(form, i, r):
                return cf[form, i, kk, r + HALO]

            def face_y(form, r, a, s_a, b, s_b):
                return (coef(form, 4, r) * a + coef(form, 5, r) * s_a) + (coef(form, 6, r) * b + coef(form, 7, r) * s_b)

            start = []
            for g in range(5):
                q = [tile(src, g, kk, first + i) for i in (-2, -1, 0, 1)]
                d = [q[i + 1] - q[i] for i in range(3)]
                s = [minmod(d[0], d[1]), minmod(d[1], d[2])]
                start.append((q[2], q[3], d[2], s[1], face_y(g // 4, first - 1, q[1], s[0], q[2], s[1])))

            def one(r, state):
                result, after = [], []
                for g in range(5):
                    form = g // 4
                    c, c_n, d_n, s, g_s = state[g]
                    c_nn = tile(src, g, kk, r + 2)
                    d_nn = c_nn - c_n
                    s_n = minmod(d_nn, d_n)
                    g_n = face_y(form, r, c, s, c_n, s_n)
                    d_e = lanes(c, -1) - c
                    s_x = minmod(d_e, lanes(d_e, 1))
                    right = coef(form, 0, r) * c + coef(form, 1, r) * s_x
                    left = coef(form, 2, r) * c + coef(form, 3, r) * s_x
                    new = c - ((right + lanes(left, -1)) - (lanes(right, 1) + left)) - (g_n - g_s)
                    result.append(new)
                    after.append((c_n, c_nn, d_nn, s_n, g_n))
                if finish:
                    total = jnp.zeros((8, width), F32)
                    for g in range(4):
                        new = jnp.where(lane < 4, lanes(result[4], -(32 * g + 8)), result[g])
                        new = jnp.where(lane >= width - 4, lanes(result[4], width - 24 - 32 * g), new)
                        dst[g, kk, pl.ds(pl.multiple_of(8 * (r + HALO), 8), 8), :] = new
                        total = total + uptakes[g] * jnp.abs(new)
                    ab[kk, pl.ds(r, 1), :] = jnp.sum(total, axis=0, keepdims=True)
                else:
                    for g in range(5):
                        dst[g, kk, pl.ds(pl.multiple_of(8 * (r + HALO), 8), 8), :] = result[g]
                return tuple(after)

            def some(i, state):
                for j in range(UNROLL):
                    state = one(first + UNROLL * i + j, state)
                return state

            lax.fori_loop(0, count // UNROLL, some, tuple(start))

    def layer(kk, first, count):
        dep = vs[1, 5, pl.ds(8 + first, count)]
        wet = wet_of((2 * t + kk).astype(F32), dep)
        return 0.25 * (0.2 + ab[kk, pl.ds(first, count)]) * wet, wet

    def send_layers(c):
        first, count = CHUNKS[c]
        s_own[c, 0:count] = layer(0, first, count)[0] + layer(1, first, count)[0]
        return [
            go(remote(s_own.at[c], s_got.at[c, d], s_s.at[c, d], s_r.at[c, d], {"trc": other[d]}))
            for d in range(3)
        ]

    def finish_chunk(c):
        first, count = CHUNKS[c]
        above = jnp.zeros((count, width), F32)
        for d in range(3):
            above = above + jnp.where(t - (d + 1) >= 0, 1.0, 0.0) * s_got[c, d, 0:count]
        light_in = surface[8 + first : 8 + first + count]
        part = pl.ds(first, count)
        for kk in range(2):
            lay, wet = layer(kk, first, count)
            over = light_in * jnp.exp(-above)
            o_t[kk, part] = th_in[kk, part] + over * (1.0 - jnp.exp(-lay))
            fl[kk, part] = DT * wet * (over / (over + 0.5))
            w01[kk, part] = DT * wet
            above = above + lay
        matrix = table[...]

        @pl.loop(0, count // 4)
        def _(i):
            for kk in range(2):
                r0 = first + 4 * i
                stacked = jnp.concatenate(
                    [jnp.concatenate([tile(c2, g, kk, r0 + j) for g in range(4)], axis=0) for j in range(4)], axis=1
                )
                mixed = jnp.dot(matrix, stacked, precision=lax.Precision.HIGHEST, preferred_element_type=F32)
                for j in range(4):
                    light = fl[kk, pl.ds(r0 + j, 1), :]
                    wet = w01[kk, pl.ds(r0 + j, 1), :]
                    for g in range(4):
                        moved = tile(c2, g, kk, r0 + j)
                        mix = mixed[8 * g : 8 * g + 8, width * j : width * (j + 1)]
                        out[g, kk, pl.ds(pl.multiple_of(8 * (r0 + j), 8), 8), :] = (
                            moved + wet * mix + light * (prod[g] * moved)
                        )

        part8 = pl.ds(8 * first, 8 * count)
        copies = [
            go(remote(out.at[other[d], :, part8], ry.at[t, :, part8], out_s.at[c, d], out_r.at[c, d], {"trc": other[d]}))
            for d in (1, 0, 2)
        ]
        here = pltpu.make_async_copy(out.at[t, :, part8], ry.at[t, :, part8], loc.at[c])
        here.start()
        return copies, here

    zero_tile = jnp.zeros((8, width), F32)
    done_pieces, done_quads = 2, 1
    layers = [None] * len(CHUNKS)
    results = [None] * len(CHUNKS)
    c1_done = -2
    stage_no = 0
    for c, (first, count) in enumerate(CHUNKS):
        quads = []
        for p in range(done_pieces, need[c]):
            for d in range(3):
                incoming[d, p].wait_recv()
            begin, size = pieces[p]
            quads = list(range(begin // 4, (begin + size) // 4))
        done_pieces = need[c]
        if quads:
            for q in quads:
                pack(q)
            pk = send_pack(c + 1, quads)
        if c > 0:
            for copy in layers[c - 1]:
                copy.wait_recv()
            results[c - 1] = finish_chunk(c - 1)
        if quads:
            for copy in pk:
                copy.wait_recv()
            for q in quads:
                strips(q)
        end = first + count + 2
        if c == 0:
            lat[0].wait_recv()

            @pl.when(la == 0)
            def _():
                for g in range(5):
                    for kk in range(2):
                        for r in range(HALO):
                            c0[g, kk, 8 * r : 8 * r + 8] = zero_tile

        if c == len(CHUNKS) - 1:
            lat[1].wait_recv()

            @pl.when(la == n_lat - 1)
            def _():
                for g in range(5):
                    for kk in range(2):
                        for r in range(rows + HALO, rows + 2 * HALO):
                            c0[g, kk, 8 * r : 8 * r + 8] = zero_tile

        step(c0, c1, c1_done, end - c1_done, False)
        c1_done = end
        step(c1, c2, first, count, True)
        layers[c] = send_layers(c)

        if c == 0:
            stage.wait_recv()
            h1[1, own] = h_in[...] - (DT * 0.5) * (dp[1] + dp_got[1])
            edges = [
                go(remote(h1.at[1, own], h1.at[0, own], h_s.at[0], h_r.at[0], {"lon": east})),
                go(remote(h1.at[1, own], h1.at[2, own], h_s.at[1], h_r.at[1], {"lon": west})),
                go(remote(h1.at[1, top], h1.at[1, pl.ds(0, 8)], h_s.at[2], h_r.at[2], {"lat": north})),
                go(remote(h1.at[1, low], h1.at[1, pl.ds(rows + 8, 8)], h_s.at[3], h_r.at[3], {"lat": south})),
            ]

    for copy in layers[-1]:
        copy.wait_recv()
    results[-1] = finish_chunk(len(CHUNKS) - 1)

    for copy in edges:
        copy.wait_recv()

    @pl.when(la == 0)
    def _():
        h1[1, 0:8] = jnp.zeros((8, width), F32)

    @pl.when(la == n_lat - 1)
    def _():
        h1[1, rows + 8 : rows + 16] = jnp.zeros((8, width), F32)

    for b in (0, 2):
        h1[b, 0:8] = jnp.zeros((8, width), F32)
        h1[b, rows + 8 : rows + 16] = jnp.zeros((8, width), F32)
    wide_h = jnp.concatenate([h1[0], h1[1], h1[2]], axis=1)
    div = jnp.zeros((rows, width), F32)
    for kk in range(2):
        u, v = mom[kk], mom[2 + kk]
        div = div + divergence(u, v)
        new_u, new_v = momentum(u, v, wide_h, wet_of((2 * t + kk).astype(F32), wide_depth))
        o_u[kk] = new_u[8 : 8 + rows, width : 2 * width]
        o_v[kk] = new_v[8 : 8 + rows, width : 2 * width]
    dp[2] = div
    stage = dp_stage(2)
    stage.wait_recv()
    dp[3] = dp[2] + dp_got[2]
    stage = dp_stage(3)

    def unturn(src, first, count):
        for kk in range(2):
            for n in range(8):
                o_x[n, 2 * src + kk, pl.ds(first, count)] = ry[src, kk, pl.ds(8 * first + n, count, stride=8), :]

    unpacked = 0
    for c, (first, count) in enumerate(CHUNKS):
        copies, here = results[c]
        here.wait()
        end = (first + count) // 8 * 8
        unturn(t, unpacked, end - unpacked)
        for copy, d in zip(copies, (1, 0, 2)):
            copy.wait_recv()
            unturn(source[d], unpacked, end - unpacked)
        unpacked = end
        if c == 0:
            stage.wait_recv()
            o_h[...] = h1[1, own] - (DT * 0.5) * (dp[3] + dp_got[3])
    for copy in sends:
        copy.wait_send()


def body(x, u, v, th, h, w, table, pace, uptake):
    tracers, levels, rows, width = x.shape
    vmem, smem = pl.BlockSpec(memory_space=pltpu.VMEM), pl.BlockSpec(memory_space=pltpu.SMEM)
    ext = rows + 2 * HALO
    n_c = len(CHUNKS)
    n_p = len(in_pieces(rows)[0])
    most = -(-max(count for _, count in CHUNKS) // 8) * 8
    dma = lambda *s: pltpu.SemaphoreType.DMA(s)
    buf = lambda *s: pltpu.VMEM(s, F32)
    scratch = [
        buf(3, 2, 8 * rows, width),
        buf(5, 2, 8 * ext, width),
        buf(5, 2, 8 * ext, width),
        buf(5, 2, 8 * ext, width),
        buf(4, 2, 8 * rows, width),
        buf(4, 2, 8 * rows, width),
        buf(2, 2, rows // 4, 8, width),
        buf(2, 2, rows // 4, 8, width),
        buf(2, 8, 2, rows + 16, width),
        buf(2, 8, 2, ext, 8, width),
        buf(3, 6, rows + 16, width),
        buf(4, rows + 16, 3 * width),
        buf(4, rows, width),
        buf(4, rows, width),
        buf(3, rows + 16, width),
        buf(2, rows, width),
        buf(n_c, most, width),
        buf(n_c, 3, most, width),
        buf(2, rows, width),
        buf(2, rows, width),
        buf(4, 8, width),
        dma(3, n_p), dma(3, n_p),
        dma(2, n_c + 1), dma(2, n_c + 1),
        dma(2), dma(2),
        dma(4), dma(4),
        dma(4), dma(4),
        dma(4), dma(4),
        dma(n_c, 3), dma(n_c, 3),
        dma(n_c, 3), dma(n_c, 3),
        dma(n_c),
    ]
    field = jax.ShapeDtypeStruct(u.shape, F32)
    return pl.pallas_call(
        kernel,
        out_shape=(
            jax.ShapeDtypeStruct(x.shape, F32), field, field, field, jax.ShapeDtypeStruct(h.shape, F32),
        ),
        in_specs=[vmem] * 7 + [smem] * 2,
        out_specs=(vmem,) * 5,
        scratch_shapes=scratch,
        compiler_params=pltpu.CompilerParams(
            collective_id=0, has_side_effects=True, vmem_limit_bytes=48 * 1024 * 1024
        ),
    )(x, u, v, th, h, w, table, pace, uptake)


def solution(mesh):
    return jax.shard_map(
        body,
        mesh=mesh,
        in_specs=(
            P("trc", None, "lat", "lon"),
            P("trc", "lat", "lon"),
            P("trc", "lat", "lon"),
            P("trc", "lat", "lon"),
            P("lat", "lon"),
            P("lat", "lon"),
            P(),
            P(),
            P(),
        ),
        out_specs=(
            P("trc", None, "lat", "lon"),
            P("trc", "lat", "lon"),
            P("trc", "lat", "lon"),
            P("trc", "lat", "lon"),
            P("lat", "lon"),
        ),
        check_vma=False,
    )
```

```python
import functools
import math

import jax
import jax.numpy as jnp
from jax import lax
from jax.experimental import pallas as pl
from jax.experimental.pallas import tpu as pltpu
from jax.sharding import PartitionSpec as P

MESH = pl.DeviceIdType.MESH
F32 = jnp.float32
DT = 0.1
CHUNKS = ((0, 12), (12, 20))
HALO = 4
THROTTLE = True
UNROLL = 4


def in_pieces(rows):
    pieces = [(0, HALO), (rows - HALO, HALO)]
    need, done = [], HALO
    for first, count in CHUNKS:
        end = min(first + count + HALO, rows - HALO)
        if end > done:
            pieces.append((done, end - done))
            done = end
        need.append(len(pieces))
    return pieces, need


def minmod(x, y):
    return jnp.maximum(jnp.minimum(x, y), jnp.minimum(jnp.maximum(x, y), 0.0))


def lanes(x, shift):
    shift = shift % x.shape[-1]
    return pltpu.roll(x, shift, x.ndim - 1) if shift else x


def rows_by(x, shift):
    shift = -shift % x.shape[0]
    return pltpu.roll(x, shift, 0) if shift else x


def kernel(
    x_far, u_far, v_far, th_far, h_far, w_far, table_far, pace, uptake,
    o_x, o_u, o_v, o_t, o_h,
    x, u_in, v_in, th_in, h_in, w_in, table,
    tx, c0, c1, c2, out, ry, pk_own, pk_got, sk, cc, cf,
    vs, mom, dp, dp_got, h1, ab, s_own, s_got, fl, w01, prod,
    ready, in_s, in_r, lon_s, lon_r, sk_s, sk_r, lat_s, lat_r, vs_s, vs_r, dp_s, dp_r, h_s, h_r,
    s_s, s_r, out_s, out_r, loc, near,
):
    rows, width = h_in.shape
    n_lat, n_lon = lax.axis_size("lat"), lax.axis_size("lon")
    t, la, lo = lax.axis_index("trc"), lax.axis_index("lat"), lax.axis_index("lon")
    other = [lax.rem(t + d, 4) for d in (1, 2, 3)]
    source = [lax.rem(t + 4 - d, 4) for d in (1, 2, 3)]
    east, west = lax.rem(lo + 1, n_lon), lax.rem(lo + n_lon - 1, n_lon)
    north, south = lax.rem(la + 1, n_lat), lax.rem(la + n_lat - 1, n_lat)
    pieces, need = in_pieces(rows)

    def remote(src, dst, send, recv, where):
        return pltpu.make_async_remote_copy(
            src_ref=src, dst_ref=dst, send_sem=send, recv_sem=recv, device_id=where, device_id_type=MESH
        )

    sends = []

    def go(copy):
        copy.start()
        sends.append(copy)
        return copy

    barrier = pltpu.get_barrier_semaphore()
    friends = [{"trc": g} for g in other] + [{"lon": west}, {"lat": north}, {"lat": south}]
    for friend in friends:
        pl.semaphore_signal(barrier, inc=1, device_id=friend, device_id_type=MESH)

    fetched = []
    for i, (far, close) in enumerate(
        ((u_far, u_in), (v_far, v_in), (h_far, h_in), (w_far, w_in), (x_far, x), (th_far, th_in), (table_far, table))
    ):
        fetched.append(pltpu.make_async_copy(far, close, near.at[i]))
        fetched[-1].start()
    for copy in fetched[:4]:
        copy.wait()

    depth = w_in[...].astype(F32)

    def wet_of(level, depths):
        return jnp.where(level < depths, 1.0, 0.0)

    own = pl.ds(8, rows)
    for kk in range(2):
        wet = wet_of((2 * t + kk).astype(F32), depth)
        vs[1, kk, own] = wet * u_in[kk]
        vs[1, 2 + kk, own] = wet * v_in[kk]
    vs[1, 4, own] = h_in[...]
    vs[1, 5, own] = depth

    lane = lax.broadcasted_iota(jnp.int32, (8, width), 1)
    slot = lane // 8
    lane32 = lane % 32
    n_half = rows // 16
    fetched[4].wait()

    @pl.loop(0, 4)
    def _(target):
        for kk in range(2):
            for n in range(8):
                tx[target, kk, pl.ds(n, rows, stride=8), :] = x[n, 2 * target + kk]

    @pl.loop(0, 4)
    def _(target):
        for kk in range(2):
            for half in range(n_half):
                to_west = to_east = jnp.zeros((8, width), F32)
                for j in range(16):
                    turned = lanes(tx[target, kk, pl.ds(8 * (16 * half + j), 8), :], 8 * (j + 1))
                    to_west = jnp.where(slot == (j + 1) % 16, turned, to_west)
                    to_east = jnp.where(slot == j, turned, to_east)
                pk_own[0, 2 * target + kk, half] = to_west
                pk_own[1, 2 * target + kk, half] = to_east

    mine = pltpu.make_async_copy(tx.at[t], c0.at[t, :, pl.ds(8 * HALO, 8 * rows)], loc.at[len(CHUNKS)])
    mine.start()
    fetched[5].wait()
    fetched[6].wait()
    pl.semaphore_wait(barrier, len(friends))
    pl.semaphore_signal(ready, inc=1, device_id={"lon": east}, device_id_type=MESH)
    vs_lon = [
        go(remote(vs.at[1, :, own], vs.at[0, :, own], vs_s.at[0], vs_r.at[0], {"lon": east})),
    ]
    pk = [go(remote(pk_own.at[1], pk_got.at[1], lon_s.at[0], lon_r.at[0], {"lon": east}))]
    incoming = {}

    def send_piece(d, p):
        first, count = pieces[p]
        incoming[d, p] = go(
            remote(
                tx.at[other[d], :, pl.ds(8 * first, 8 * count)],
                c0.at[t, :, pl.ds(8 * (first + HALO), 8 * count)],
                in_s.at[d, p], in_r.at[d, p], {"trc": other[d]},
            )
        )

    def send_pieces(p):
        if p < len(pieces):
            for d in (1, 0, 2):
                send_piece(d, p)

    send_pieces(0)
    send_pieces(1)
    send_pieces(2)
    if not THROTTLE:
        for p in range(3, len(pieces)):
            send_pieces(p)

    pl.semaphore_wait(ready, 1)
    vs_lon.append(go(remote(vs.at[1, :, own], vs.at[2, :, own], vs_s.at[1], vs_r.at[1], {"lon": west})))
    pk.append(go(remote(pk_own.at[0], pk_got.at[0], lon_s.at[1], lon_r.at[1], {"lon": west})))
    for copy in vs_lon:
        copy.wait_recv()
    top, low = pl.ds(rows, 8), pl.ds(8, 8)
    vs_lat = [
        go(remote(vs.at[:, :, top], vs.at[:, :, pl.ds(0, 8)], vs_s.at[2], vs_r.at[2], {"lat": north})),
        go(remote(vs.at[:, :, low], vs.at[:, :, pl.ds(rows + 8, 8)], vs_s.at[3], vs_r.at[3], {"lat": south})),
    ]

    for copy in pk:
        copy.wait_recv()
    strip_in = [
        go(remote(pk_got.at[:, pl.ds(2 * other[d], 2)], sk.at[:, t], sk_s.at[d], sk_r.at[d], {"trc": other[d]}))
        for d in range(3)
    ]
    mine_too = pltpu.make_async_copy(pk_got.at[:, pl.ds(2 * t, 2)], sk.at[:, t], loc.at[len(CHUNKS) + 1])
    mine_too.start()

    def tile(buf, g, kk, r):
        return buf[g, kk, pl.ds(pl.multiple_of(8 * (r + HALO), 8), 8), :]

    def strips(begin, end):
        @pl.loop(begin, end)
        def _(r):
            half, j = r // 16, r % 16
            for kk in range(2):
                strip = jnp.zeros((8, width), F32)
                for g in range(4):
                    here = tile(c0, g, kk, r)
                    parts = (
                        pltpu.roll(sk[1, g, kk, half], (32 * g + width - 8 * j) % width, 1),
                        lanes(here, 32 * g + 8),
                        lanes(here, 32 * g + 24),
                        pltpu.roll(sk[0, g, kk, half], (32 * g + 16 + width - 8 * j) % width, 1),
                    )
                    for i, part in enumerate(parts):
                        strip = jnp.where(slot == 4 * g + i, part, strip)
                c0[4, kk, pl.ds(pl.multiple_of(8 * (r + HALO), 8), 8), :] = strip

    for p in (0, 1):
        for d in range(3):
            incoming[d, p].wait_recv()
    if THROTTLE:
        send_pieces(3)
    for copy in vs_lat:
        copy.wait_recv()

    @pl.when(la == 0)
    def _():
        for b in range(3):
            for f in range(6):
                vs[b, f, 0:8] = jnp.zeros((8, width), F32)

    @pl.when(la == n_lat - 1)
    def _():
        for b in range(3):
            for f in range(6):
                vs[b, f, rows + 8 : rows + 16] = jnp.zeros((8, width), F32)

    vlane = lax.broadcasted_iota(jnp.int32, (rows + 16, width), 1) % 32

    def strip_form(f):
        w_, o_, e_ = vs[0, f], vs[1, f], vs[2, f]
        left = jnp.where(vlane < 8, lanes(w_, 8), lanes(o_, 8))
        right = jnp.where(vlane < 24, lanes(o_, 24), lanes(e_, 24))
        first = jnp.where(vlane < 16, left, right)
        lane_ = lax.broadcasted_iota(jnp.int32, first.shape, 1)
        first = jnp.where(lane_ < 32, first, 0.0)
        first = first + lanes(first, 32)
        return first + lanes(first, 64)

    def weights(a):
        ap, an = jnp.maximum(a, 0.0), jnp.minimum(a, 0.0)
        return ap, 0.5 * ap * (1.0 - ap), an, -0.5 * an * (1.0 + an)

    for form in range(2):
        get = (lambda f: vs[1, f]) if form == 0 else strip_form
        dep = get(5)
        for kk in range(2):
            wet = wet_of((2 * t + kk).astype(F32), dep)
            u, v = get(kk), get(2 + kk)
            ax = 0.5 * (u + lanes(u, -1)) * wet * lanes(wet, -1)
            ap, bp, an, bn = weights(ax)
            cc[form, 0, kk], cc[form, 1, kk] = ap, bp
            cc[form, 2, kk], cc[form, 3, kk] = lanes(an, 1), lanes(bn, 1)
            ay = 0.5 * (v + rows_by(v, 1)) * wet * rows_by(wet, 1)
            for i, w in enumerate(weights(ay)):
                cc[form, 4 + i, kk] = w

    @pl.loop(1, rows + 2 * HALO)
    def _(r):
        for form in range(2):
            for i in range(8):
                for kk in range(2):
                    cf[form, i, kk, r] = jnp.broadcast_to(cc[form, i, kk, pl.ds(r + 8 - HALO, 1), :], (8, width))

    big = rows + 16
    row_no = (la * rows - 8 + lax.broadcasted_iota(jnp.int32, (big, 1), 0)).astype(F32)
    angle = math.pi * ((row_no + 0.5) / (rows * n_lat) - 0.5)
    coriolis = 0.5 * jnp.sin(angle)
    surface = 1.0 + jnp.cos(angle)
    wide = lambda ref, f: jnp.concatenate([ref[0, f], ref[1, f], ref[2, f]], axis=1)

    def momentum(u, v, h, wet):
        h_x = 0.5 * (lanes(h, -1) - lanes(h, 1))
        h_y = 0.5 * (rows_by(h, 1) - rows_by(h, -1))
        lap_u = rows_by(u, 1) + rows_by(u, -1) + lanes(u, -1) + lanes(u, 1) - 4.0 * u
        lap_v = rows_by(v, 1) + rows_by(v, -1) + lanes(v, -1) + lanes(v, 1) - 4.0 * v
        new_u = wet * (u + DT * (coriolis * v - h_x + 0.2 * lap_u - 0.05 * u))
        new_v = wet * (v + DT * (-coriolis * u - h_y + 0.2 * lap_v - 0.05 * v))
        return new_u, new_v

    def divergence(u, v):
        d = 0.5 * (lanes(u, -1) - lanes(u, 1)) + 0.5 * (rows_by(v, 1) - rows_by(v, -1))
        return d[8 : 8 + rows, width : 2 * width]

    def dp_stage(i):
        partner = t + 1 - 2 * lax.rem(t, 2) if i % 2 == 0 else 3 - t
        return go(remote(dp.at[i], dp_got.at[i], dp_s.at[i], dp_r.at[i], {"trc": partner}))

    wide_depth = wide(vs, 5)
    wide_h = wide(vs, 4)
    div = jnp.zeros((rows, width), F32)
    for kk in range(2):
        u, v = wide(vs, kk), wide(vs, 2 + kk)
        div = div + divergence(u, v)
        mom[kk], mom[2 + kk] = momentum(u, v, wide_h, wet_of((2 * t + kk).astype(F32), wide_depth))
    dp[0] = div
    stage = dp_stage(0)

    mine.wait()
    mine_too.wait()
    for copy in strip_in:
        copy.wait_recv()
    strips(0, HALO)
    strips(rows - HALO, rows)
    lat = [
        go(remote(c0.at[:, :, pl.ds(8 * rows, 8 * HALO)], c0.at[:, :, pl.ds(0, 8 * HALO)],
                  lat_s.at[0], lat_r.at[0], {"lat": north})),
        go(remote(c0.at[:, :, pl.ds(8 * HALO, 8 * HALO)], c0.at[:, :, pl.ds(8 * (rows + HALO), 8 * HALO)],
                  lat_s.at[1], lat_r.at[1], {"lat": south})),
    ]
    stage.wait_recv()
    dp[1] = dp[0] + dp_got[0]
    stage = dp_stage(1)

    sub = lax.broadcasted_iota(jnp.int32, (8, width), 0)

    def column(ref, g):
        col = jnp.full((8, width), ref[8 * g], F32)
        for n in range(1, 8):
            col = jnp.where(sub == n, ref[8 * g + n], col)
        return col

    uptakes = [column(uptake, g) for g in range(4)]
    for g in range(4):
        prod[g] = column(pace, g)

    def step(src, dst, first, count, finish):
        @pl.loop(0, 2)
        def _(kk):
            def coef(form, i, r):
                return cf[form, i, kk, r + HALO]

            def face_y(form, r, a, s_a, b, s_b):
                return (coef(form, 4, r) * a + coef(form, 5, r) * s_a) + (coef(form, 6, r) * b + coef(form, 7, r) * s_b)

            start = []
            for g in range(5):
                q = [tile(src, g, kk, first + i) for i in (-2, -1, 0, 1)]
                d = [q[i + 1] - q[i] for i in range(3)]
                s = [minmod(d[0], d[1]), minmod(d[1], d[2])]
                start.append((q[2], q[3], d[2], s[1], face_y(g // 4, first - 1, q[1], s[0], q[2], s[1])))

            def one(r, state):
                result, after = [], []
                for g in range(5):
                    form = g // 4
                    c, c_n, d_n, s, g_s = state[g]
                    c_nn = tile(src, g, kk, r + 2)
                    d_nn = c_nn - c_n
                    s_n = minmod(d_nn, d_n)
                    g_n = face_y(form, r, c, s, c_n, s_n)
                    d_e = lanes(c, -1) - c
                    s_x = minmod(d_e, lanes(d_e, 1))
                    right = coef(form, 0, r) * c + coef(form, 1, r) * s_x
                    left = coef(form, 2, r) * c + coef(form, 3, r) * s_x
                    new = c - ((right + lanes(left, -1)) - (lanes(right, 1) + left)) - (g_n - g_s)
                    result.append(new)
                    after.append((c_n, c_nn, d_nn, s_n, g_n))
                if finish:
                    total = jnp.zeros((8, width), F32)
                    for g in range(4):
                        new = jnp.where(lane < 4, lanes(result[4], -(32 * g + 8)), result[g])
                        new = jnp.where(lane >= width - 4, lanes(result[4], width - 24 - 32 * g), new)
                        dst[g, kk, pl.ds(pl.multiple_of(8 * (r + HALO), 8), 8), :] = new
                        total = total + uptakes[g] * jnp.abs(new)
                    ab[kk, pl.ds(r, 1), :] = jnp.sum(total, axis=0, keepdims=True)
                else:
                    for g in range(5):
                        dst[g, kk, pl.ds(pl.multiple_of(8 * (r + HALO), 8), 8), :] = result[g]
                return tuple(after)

            def some(i, state):
                for j in range(UNROLL):
                    state = one(first + UNROLL * i + j, state)
                return state

            lax.fori_loop(0, count // UNROLL, some, tuple(start))

    def layer(kk, first, count):
        dep = vs[1, 5, pl.ds(8 + first, count)]
        wet = wet_of((2 * t + kk).astype(F32), dep)
        return 0.25 * (0.2 + ab[kk, pl.ds(first, count)]) * wet, wet

    def send_layers(c):
        first, count = CHUNKS[c]
        s_own[c, 0:count] = layer(0, first, count)[0] + layer(1, first, count)[0]
        return [
            go(remote(s_own.at[c], s_got.at[c, d], s_s.at[c, d], s_r.at[c, d], {"trc": other[d]}))
            for d in range(3)
        ]

    def finish_chunk(c):
        first, count = CHUNKS[c]
        above = jnp.zeros((count, width), F32)
        for d in range(3):
            above = above + jnp.where(t - (d + 1) >= 0, 1.0, 0.0) * s_got[c, d, 0:count]
        light_in = surface[8 + first : 8 + first + count]
        part = pl.ds(first, count)
        for kk in range(2):
            lay, wet = layer(kk, first, count)
            over = light_in * jnp.exp(-above)
            o_t[kk, part] = th_in[kk, part] + over * (1.0 - jnp.exp(-lay))
            fl[kk, part] = DT * wet * (over / (over + 0.5))
            w01[kk, part] = DT * wet
            above = above + lay
        matrix = table[...]

        @pl.loop(0, count // 4)
        def _(i):
            for kk in range(2):
                r0 = first + 4 * i
                stacked = jnp.concatenate(
                    [jnp.concatenate([tile(c2, g, kk, r0 + j) for g in range(4)], axis=0) for j in range(4)], axis=1
                )
                mixed = jnp.dot(matrix, stacked, precision=lax.Precision.HIGHEST, preferred_element_type=F32)
                for j in range(4):
                    light = fl[kk, pl.ds(r0 + j, 1), :]
                    wet = w01[kk, pl.ds(r0 + j, 1), :]
                    for g in range(4):
                        moved = tile(c2, g, kk, r0 + j)
                        mix = mixed[8 * g : 8 * g + 8, width * j : width * (j + 1)]
                        out[g, kk, pl.ds(pl.multiple_of(8 * (r0 + j), 8), 8), :] = (
                            moved + wet * mix + light * (prod[g] * moved)
                        )

        part8 = pl.ds(8 * first, 8 * count)
        copies = [
            go(remote(out.at[other[d], :, part8], ry.at[t, :, part8], out_s.at[c, d], out_r.at[c, d], {"trc": other[d]}))
            for d in (1, 0, 2)
        ]
        here = pltpu.make_async_copy(out.at[t, :, part8], ry.at[t, :, part8], loc.at[c])
        here.start()
        return copies, here

    zero_tile = jnp.zeros((8, width), F32)
    done_pieces = 2
    layers = [None] * len(CHUNKS)
    results = [None] * len(CHUNKS)
    c1_done = -2
    stage_no = 0
    for c, (first, count) in enumerate(CHUNKS):
        for p in range(done_pieces, need[c]):
            for d in range(3):
                incoming[d, p].wait_recv()
            begin, size = pieces[p]
            if THROTTLE:
                send_pieces(p + 2)
            strips(begin, begin + size)
        done_pieces = need[c]
        if c > 0:
            for copy in layers[c - 1]:
                copy.wait_recv()
            results[c - 1] = finish_chunk(c - 1)
        end = first + count + 2
        if c == 0:
            lat[0].wait_recv()

            @pl.when(la == 0)
            def _():
                for g in range(5):
                    for kk in range(2):
                        for r in range(HALO):
                            c0[g, kk, 8 * r : 8 * r + 8] = zero_tile

        if c == len(CHUNKS) - 1:
            lat[1].wait_recv()

            @pl.when(la == n_lat - 1)
            def _():
                for g in range(5):
                    for kk in range(2):
                        for r in range(rows + HALO, rows + 2 * HALO):
                            c0[g, kk, 8 * r : 8 * r + 8] = zero_tile

        step(c0, c1, c1_done, end - c1_done, False)
        c1_done = end
        step(c1, c2, first, count, True)
        layers[c] = send_layers(c)

        if c == 0:
            stage.wait_recv()
            h1[1, own] = h_in[...] - (DT * 0.5) * (dp[1] + dp_got[1])
            edges = [
                go(remote(h1.at[1, own], h1.at[0, own], h_s.at[0], h_r.at[0], {"lon": east})),
                go(remote(h1.at[1, own], h1.at[2, own], h_s.at[1], h_r.at[1], {"lon": west})),
                go(remote(h1.at[1, top], h1.at[1, pl.ds(0, 8)], h_s.at[2], h_r.at[2], {"lat": north})),
                go(remote(h1.at[1, low], h1.at[1, pl.ds(rows + 8, 8)], h_s.at[3], h_r.at[3], {"lat": south})),
            ]

    for copy in edges:
        copy.wait_recv()

    @pl.when(la == 0)
    def _():
        h1[1, 0:8] = jnp.zeros((8, width), F32)

    @pl.when(la == n_lat - 1)
    def _():
        h1[1, rows + 8 : rows + 16] = jnp.zeros((8, width), F32)

    for b in (0, 2):
        h1[b, 0:8] = jnp.zeros((8, width), F32)
        h1[b, rows + 8 : rows + 16] = jnp.zeros((8, width), F32)
    wide_h = jnp.concatenate([h1[0], h1[1], h1[2]], axis=1)
    div = jnp.zeros((rows, width), F32)
    for kk in range(2):
        u, v = mom[kk], mom[2 + kk]
        div = div + divergence(u, v)
        new_u, new_v = momentum(u, v, wide_h, wet_of((2 * t + kk).astype(F32), wide_depth))
        o_u[kk] = new_u[8 : 8 + rows, width : 2 * width]
        o_v[kk] = new_v[8 : 8 + rows, width : 2 * width]
    dp[2] = div
    stage = dp_stage(2)
    for copy in layers[-1]:
        copy.wait_recv()
    results[-1] = finish_chunk(len(CHUNKS) - 1)

    stage.wait_recv()
    dp[3] = dp[2] + dp_got[2]
    stage = dp_stage(3)

    def unturn(src, first, count):
        for kk in range(2):
            for n in range(8):
                o_x[n, 2 * src + kk, pl.ds(first, count)] = ry[src, kk, pl.ds(8 * first + n, count, stride=8), :]

    unpacked = 0
    for c, (first, count) in enumerate(CHUNKS):
        copies, here = results[c]
        here.wait()
        end = (first + count) // 8 * 8
        unturn(t, unpacked, end - unpacked)
        for copy, d in zip(copies, (1, 0, 2)):
            copy.wait_recv()
            unturn(source[d], unpacked, end - unpacked)
        unpacked = end
        if c == 0:
            stage.wait_recv()
            o_h[...] = h1[1, own] - (DT * 0.5) * (dp[3] + dp_got[3])
    for copy in sends:
        copy.wait_send()


def place(*refs):
    far, to, near, come, leave = refs[:5], refs[5:10], refs[10:15], refs[15], refs[16]
    moves = []
    for i in range(5):
        parts = [slice(None)] if i else [pl.ds(2 * p, 2) for p in range(4)]
        for part in parts:
            n = len(moves)
            moves.append(
                (
                    pltpu.make_async_copy(far[i].at[part], near[i].at[part], come.at[n]),
                    pltpu.make_async_copy(near[i].at[part], to[i].at[part], leave.at[n]),
                )
            )
    for first, _ in moves:
        first.start()
    for first, second in moves:
        first.wait()
        second.start()
    for _, second in moves:
        second.wait()


def body(x, u, v, th, h, w, table, pace, uptake):
    tracers, levels, rows, width = x.shape
    vmem, smem = pl.BlockSpec(memory_space=pltpu.VMEM), pl.BlockSpec(memory_space=pltpu.SMEM)
    ext = rows + 2 * HALO
    n_c = len(CHUNKS)
    n_p = len(in_pieces(rows)[0])
    most = -(-max(count for _, count in CHUNKS) // 8) * 8
    dma = lambda *s: pltpu.SemaphoreType.DMA(s)
    buf = lambda *s: pltpu.VMEM(s, F32)
    scratch = [
        *(pltpu.VMEM(a.shape, a.dtype) for a in (x, u, v, th, h, w, table)),
        buf(4, 2, 8 * rows, width),
        buf(5, 2, 8 * ext, width),
        buf(5, 2, 8 * ext, width),
        buf(5, 2, 8 * ext, width),
        buf(4, 2, 8 * rows, width),
        buf(4, 2, 8 * rows, width),
        buf(2, 8, rows // 16, 8, width),
        buf(2, 8, rows // 16, 8, width),
        buf(2, 4, 2, rows // 16, 8, width),
        buf(2, 8, 2, rows + 16, width),
        buf(2, 8, 2, ext, 8, width),
        buf(3, 6, rows + 16, width),
        buf(4, rows + 16, 3 * width),
        buf(4, rows, width),
        buf(4, rows, width),
        buf(3, rows + 16, width),
        buf(2, rows, width),
        buf(n_c, most, width),
        buf(n_c, 3, most, width),
        buf(2, rows, width),
        buf(2, rows, width),
        buf(4, 8, width),
        pltpu.SemaphoreType.REGULAR,
        dma(3, n_p), dma(3, n_p),
        dma(2), dma(2),
        dma(3), dma(3),
        dma(2), dma(2),
        dma(4), dma(4),
        dma(4), dma(4),
        dma(4), dma(4),
        dma(n_c, 3), dma(n_c, 3),
        dma(n_c, 3), dma(n_c, 3),
        dma(n_c + 2), dma(7),
    ]
    field = jax.ShapeDtypeStruct(u.shape, F32)
    results = pl.pallas_call(
        kernel,
        out_shape=(
            jax.ShapeDtypeStruct(x.shape, F32), field, field, field, jax.ShapeDtypeStruct(h.shape, F32),
        ),
        in_specs=[pl.BlockSpec(memory_space=pltpu.HBM)] * 7 + [smem] * 2,
        out_specs=(vmem,) * 5,
        scratch_shapes=scratch,
        compiler_params=pltpu.CompilerParams(
            collective_id=0, has_side_effects=True, vmem_limit_bytes=62 * 1024 * 1024
        ),
    )(x, u, v, th, h, w, table, pace, uptake)

    return pl.pallas_call(
        place,
        out_shape=tuple(jax.ShapeDtypeStruct(r.shape, F32) for r in results),
        in_specs=[pl.BlockSpec(memory_space=pltpu.HBM)] * 5,
        out_specs=(pl.BlockSpec(memory_space=pltpu.HBM),) * 5,
        scratch_shapes=[*(pltpu.VMEM(r.shape, F32) for r in results), dma(8), dma(8)],
        compiler_params=pltpu.CompilerParams(vmem_limit_bytes=62 * 1024 * 1024),
    )(*results)


def solution(mesh):
    return jax.shard_map(
        body,
        mesh=mesh,
        in_specs=(
            P("trc", None, "lat", "lon"),
            P("trc", "lat", "lon"),
            P("trc", "lat", "lon"),
            P("trc", "lat", "lon"),
            P("lat", "lon"),
            P("lat", "lon"),
            P(),
            P(),
            P(),
        ),
        out_specs=(
            P("trc", None, "lat", "lon"),
            P("trc", "lat", "lon"),
            P("trc", "lat", "lon"),
            P("trc", "lat", "lon"),
            P("lat", "lon"),
        ),
        check_vma=False,
    )
```

```python
import functools
import math

import jax
import jax.numpy as jnp
from jax import lax
from jax.experimental import pallas as pl
from jax.experimental.pallas import tpu as pltpu
from jax.sharding import PartitionSpec as P

MESH = pl.DeviceIdType.MESH
F32 = jnp.float32
DT = 0.1
CHUNKS = ((0, 16), (16, 16))
PARTS = (((0, 8), (8, 8)), ((16, 8), (24, 8)))
N_PARTS = sum(len(p) for p in PARTS)
HALO = 4
THROTTLE = True
ROUNDS = 2
GROUPS = ((0, 1, 2, 3, 4),)


def in_pieces(rows):
    pieces = [(0, HALO), (rows - HALO, HALO)]
    need, done = [], HALO
    for first, count in CHUNKS:
        end = min(first + count + HALO, rows - HALO)
        if end > done:
            pieces.append((done, end - done))
            done = end
        need.append(len(pieces))
    return pieces, need


def minmod(x, y):
    return jnp.maximum(jnp.minimum(x, y), jnp.minimum(jnp.maximum(x, y), 0.0))


def lanes(x, shift):
    shift = shift % x.shape[-1]
    return pltpu.roll(x, shift, x.ndim - 1) if shift else x


def rows_by(x, shift):
    shift = -shift % x.shape[0]
    return pltpu.roll(x, shift, 0) if shift else x


def kernel(
    x_far, u_far, v_far, th_far, h_far, w_far, table_far, pace, uptake,
    far_x, far_u, far_v, far_t, far_h,
    o_x, o_u, o_v, o_t, o_h,
    x, u_in, v_in, th_in, h_in, w_in, table,
    tx, c0, c1, c2, out, ry, pk_own, pk_got, sk, cc, cf,
    vs, ve_own, ve_got, mom, dp, dp_got, h1, ab, s_own, s_got, fl, w01, prod,
    ready, in_s, in_r, lon_s, lon_r, sk_s, sk_r, lat_s, lat_r, vs_s, vs_r, dp_s, dp_r, h_s, h_r,
    s_s, s_r, out_s, out_r, loc, near, away,
):
    rows, width = h_in.shape
    n_lat, n_lon = lax.axis_size("lat"), lax.axis_size("lon")
    t, la, lo = lax.axis_index("trc"), lax.axis_index("lat"), lax.axis_index("lon")
    other = [lax.rem(t + d, 4) for d in (1, 2, 3)]
    source = [lax.rem(t + 4 - d, 4) for d in (1, 2, 3)]
    east, west = lax.rem(lo + 1, n_lon), lax.rem(lo + n_lon - 1, n_lon)
    north, south = lax.rem(la + 1, n_lat), lax.rem(la + n_lat - 1, n_lat)
    pieces, need = in_pieces(rows)

    def remote(src, dst, send, recv, where):
        return pltpu.make_async_remote_copy(
            src_ref=src, dst_ref=dst, send_sem=send, recv_sem=recv, device_id=where, device_id_type=MESH
        )

    sends = []

    def go(copy):
        copy.start()
        sends.append(copy)
        return copy

    barrier = pltpu.get_barrier_semaphore()
    friends = [{"trc": g} for g in other] + [{"lon": west}, {"lat": north}, {"lat": south}]
    for friend in friends:
        pl.semaphore_signal(barrier, inc=1, device_id=friend, device_id_type=MESH)

    fetched = []
    for i, (far, close) in enumerate(
        ((u_far, u_in), (v_far, v_in), (h_far, h_in), (w_far, w_in), (x_far, x), (th_far, th_in), (table_far, table))
    ):
        fetched.append(pltpu.make_async_copy(far, close, near.at[i]))
        fetched[-1].start()
    for copy in fetched[:4]:
        copy.wait()

    depth = w_in[...].astype(F32)

    def wet_of(level, depths):
        return jnp.where(level < depths, 1.0, 0.0)

    own = pl.ds(8, rows)
    for kk in range(2):
        wet = wet_of((2 * t + kk).astype(F32), depth)
        vs[1, kk, own] = wet * u_in[kk]
        vs[1, 2 + kk, own] = wet * v_in[kk]
    vs[1, 4, own] = h_in[...]
    vs[1, 5, own] = depth

    lane = lax.broadcasted_iota(jnp.int32, (8, width), 1)
    slot = lane // 8
    lane32 = lane % 32
    slot4 = lane // 4
    fetched[4].wait()

    @pl.loop(0, 4)
    def _(target):
        for kk in range(2):
            fields = [x[n, 2 * target + kk] for n in range(8)]
            for n in range(8):
                tx[target, kk, pl.ds(n, rows, stride=8), :] = fields[n]

    @pl.loop(0, 4)
    def _(target):
        for kk in range(2):
            to_west = to_east = jnp.zeros((8, width), F32)
            for j in range(rows):
                turned = lanes(tx[target, kk, pl.ds(8 * j, 8), :], 4 * (j + 1))
                to_west = jnp.where(slot4 == (j + 1) % 32, turned, to_west)
                to_east = jnp.where(slot4 == j, turned, to_east)
            pk_own[0, 2 * target + kk] = to_west
            pk_own[1, 2 * target + kk] = to_east

    lane_v = lax.broadcasted_iota(jnp.int32, (rows, width), 1) // 8
    to_west = to_east = jnp.zeros((rows, width), F32)
    for f in range(6):
        field = vs[1, f, own]
        to_west = jnp.where(lane_v == f, lanes(field, 8 * f), to_west)
        to_east = jnp.where(lane_v == f, lanes(field, 8 * f + 8), to_east)
    ve_own[0], ve_own[1] = to_west, to_east

    mine = pltpu.make_async_copy(tx.at[t], c0.at[t, :, pl.ds(8 * HALO, 8 * rows)], loc.at[N_PARTS])
    mine.start()
    fetched[5].wait()
    fetched[6].wait()
    pl.semaphore_wait(barrier, len(friends))
    pl.semaphore_signal(ready, inc=1, device_id={"lon": east}, device_id_type=MESH)
    vs_lon = [
        go(remote(ve_own.at[1], ve_got.at[1], vs_s.at[0], vs_r.at[0], {"lon": east})),
    ]
    pk = [go(remote(pk_own.at[1], pk_got.at[1], lon_s.at[0], lon_r.at[0], {"lon": east}))]
    incoming = {}

    def send_piece(d, p):
        first, count = pieces[p]
        incoming[d, p] = go(
            remote(
                tx.at[other[d], :, pl.ds(8 * first, 8 * count)],
                c0.at[t, :, pl.ds(8 * (first + HALO), 8 * count)],
                in_s.at[d, p], in_r.at[d, p], {"trc": other[d]},
            )
        )

    def send_pieces(p):
        if p < len(pieces):
            for d in (1, 0, 2):
                send_piece(d, p)

    send_pieces(0)
    send_pieces(1)
    send_pieces(2)
    if not THROTTLE:
        for p in range(3, len(pieces)):
            send_pieces(p)

    pl.semaphore_wait(ready, 1)
    vs_lon.append(go(remote(ve_own.at[0], ve_got.at[0], vs_s.at[1], vs_r.at[1], {"lon": west})))
    pk.append(go(remote(pk_own.at[0], pk_got.at[0], lon_s.at[1], lon_r.at[1], {"lon": west})))
    for copy in vs_lon:
        copy.wait_recv()
    for f in range(6):
        vs[0, f, own] = lanes(ve_got[1], width - 8 - 8 * f)
        vs[2, f, own] = lanes(ve_got[0], -8 * f)
    top, low = pl.ds(rows, 8), pl.ds(8, 8)
    vs_lat = [
        go(remote(vs.at[:, :, top], vs.at[:, :, pl.ds(0, 8)], vs_s.at[2], vs_r.at[2], {"lat": north})),
        go(remote(vs.at[:, :, low], vs.at[:, :, pl.ds(rows + 8, 8)], vs_s.at[3], vs_r.at[3], {"lat": south})),
    ]

    for copy in pk:
        copy.wait_recv()
    strip_in = [
        go(remote(pk_got.at[:, pl.ds(2 * other[d], 2)], sk.at[:, t], sk_s.at[d], sk_r.at[d], {"trc": other[d]}))
        for d in range(3)
    ]
    mine_too = pltpu.make_async_copy(pk_got.at[:, pl.ds(2 * t, 2)], sk.at[:, t], loc.at[N_PARTS + 1])
    mine_too.start()

    def tile(buf, g, kk, r):
        return buf[g, kk, pl.ds(pl.multiple_of(8 * (r + HALO), 8), 8), :]

    def strips(begin, end):
        @pl.loop(0, (end - begin) // 4)
        def _(quad):
            results = []
            for i in range(4):
                r = begin + 4 * quad + i
                for kk in range(2):
                    strip = jnp.zeros((8, width), F32)
                    for g in range(4):
                        here = tile(c0, g, kk, r)
                        parts = (
                            pltpu.roll(sk[1, g, kk], (32 * g + 4 + width - 4 * r) % width, 1),
                            lanes(here, 32 * g + 8),
                            lanes(here, 32 * g + 24),
                            pltpu.roll(sk[0, g, kk], (32 * g + 20 + width - 4 * r) % width, 1),
                        )
                        for n, part in enumerate(parts):
                            strip = jnp.where(slot == 4 * g + n, part, strip)
                    results.append(strip)
            for i in range(4):
                for kk in range(2):
                    put = pl.ds(pl.multiple_of(8 * (begin + 4 * quad + i + HALO), 8), 8)
                    c0[4, kk, put, :] = results[2 * i + kk]

    for p in (0, 1):
        for d in range(3):
            incoming[d, p].wait_recv()
    if THROTTLE:
        send_pieces(3)
    mine.wait()
    mine_too.wait()
    for copy in strip_in:
        copy.wait_recv()
    strips(0, HALO)
    strips(rows - HALO, rows)
    lat = [
        go(remote(c0.at[:, :, pl.ds(8 * rows, 8 * HALO)], c0.at[:, :, pl.ds(0, 8 * HALO)],
                  lat_s.at[0], lat_r.at[0], {"lat": north})),
        go(remote(c0.at[:, :, pl.ds(8 * HALO, 8 * HALO)], c0.at[:, :, pl.ds(8 * (rows + HALO), 8 * HALO)],
                  lat_s.at[1], lat_r.at[1], {"lat": south})),
    ]
    for copy in vs_lat:
        copy.wait_recv()

    @pl.when(la == 0)
    def _():
        for b in range(3):
            for f in range(6):
                vs[b, f, 0:8] = jnp.zeros((8, width), F32)

    @pl.when(la == n_lat - 1)
    def _():
        for b in range(3):
            for f in range(6):
                vs[b, f, rows + 8 : rows + 16] = jnp.zeros((8, width), F32)

    vlane = lax.broadcasted_iota(jnp.int32, (rows + 16, width), 1) % 32

    def strip_form(f):
        w_, o_, e_ = vs[0, f], vs[1, f], vs[2, f]
        left = jnp.where(vlane < 8, lanes(w_, 8), lanes(o_, 8))
        right = jnp.where(vlane < 24, lanes(o_, 24), lanes(e_, 24))
        first = jnp.where(vlane < 16, left, right)
        lane_ = lax.broadcasted_iota(jnp.int32, first.shape, 1)
        first = jnp.where(lane_ < 32, first, 0.0)
        first = first + lanes(first, 32)
        return first + lanes(first, 64)

    def weights(a):
        ap, an = jnp.maximum(a, 0.0), jnp.minimum(a, 0.0)
        return ap, 0.5 * ap * (1.0 - ap), an, -0.5 * an * (1.0 + an)

    for form in range(2):
        get = (lambda f: vs[1, f]) if form == 0 else strip_form
        dep = get(5)
        for kk in range(2):
            wet = wet_of((2 * t + kk).astype(F32), dep)
            u, v = get(kk), get(2 + kk)
            ax = 0.5 * (u + lanes(u, -1)) * wet * lanes(wet, -1)
            ap, bp, an, bn = weights(ax)
            cc[form, 0, kk], cc[form, 1, kk] = ap, bp
            cc[form, 2, kk], cc[form, 3, kk] = lanes(an, 1), lanes(bn, 1)
            ay = 0.5 * (v + rows_by(v, 1)) * wet * rows_by(wet, 1)
            for i, w in enumerate(weights(ay)):
                cc[form, 4 + i, kk] = w

    @pl.loop(1, rows + 2 * HALO)
    def _(r):
        every = [(form, i, kk) for form in range(2) for i in range(8) for kk in range(2)]
        wide_rows = [jnp.broadcast_to(cc[f, i, kk, pl.ds(r + 8 - HALO, 1), :], (8, width)) for f, i, kk in every]
        for (f, i, kk), value in zip(every, wide_rows):
            cf[f, i, kk, r] = value

    big = rows + 16
    row_no = (la * rows - 8 + lax.broadcasted_iota(jnp.int32, (big, 1), 0)).astype(F32)
    angle = math.pi * ((row_no + 0.5) / (rows * n_lat) - 0.5)
    coriolis = 0.5 * jnp.sin(angle)
    surface = 1.0 + jnp.cos(angle)
    wide = lambda ref, f: jnp.concatenate([ref[0, f], ref[1, f], ref[2, f]], axis=1)

    def momentum(u, v, h, wet):
        h_x = 0.5 * (lanes(h, -1) - lanes(h, 1))
        h_y = 0.5 * (rows_by(h, 1) - rows_by(h, -1))
        lap_u = rows_by(u, 1) + rows_by(u, -1) + lanes(u, -1) + lanes(u, 1) - 4.0 * u
        lap_v = rows_by(v, 1) + rows_by(v, -1) + lanes(v, -1) + lanes(v, 1) - 4.0 * v
        new_u = wet * (u + DT * (coriolis * v - h_x + 0.2 * lap_u - 0.05 * u))
        new_v = wet * (v + DT * (-coriolis * u - h_y + 0.2 * lap_v - 0.05 * v))
        return new_u, new_v

    def divergence(u, v):
        d = 0.5 * (lanes(u, -1) - lanes(u, 1)) + 0.5 * (rows_by(v, 1) - rows_by(v, -1))
        return d[8 : 8 + rows, width : 2 * width]

    def dp_stage(i):
        partner = t + 1 - 2 * lax.rem(t, 2) if i % 2 == 0 else 3 - t
        return go(remote(dp.at[i], dp_got.at[i], dp_s.at[i], dp_r.at[i], {"trc": partner}))

    wide_depth = wide(vs, 5)
    wide_h = wide(vs, 4)
    div = jnp.zeros((rows, width), F32)
    for kk in range(2):
        u, v = wide(vs, kk), wide(vs, 2 + kk)
        div = div + divergence(u, v)
        mom[kk], mom[2 + kk] = momentum(u, v, wide_h, wet_of((2 * t + kk).astype(F32), wide_depth))
    dp[0] = div
    stage = dp_stage(0)

    stage.wait_recv()
    dp[1] = dp[0] + dp_got[0]
    stage = dp_stage(1)

    sub = lax.broadcasted_iota(jnp.int32, (8, width), 0)

    def column(ref, g):
        col = jnp.full((8, width), ref[8 * g], F32)
        for n in range(1, 8):
            col = jnp.where(sub == n, ref[8 * g + n], col)
        return col

    uptakes = [column(uptake, g) for g in range(4)]
    for g in range(4):
        prod[g] = column(pace, g)

    def step(src, dst, first, count):
        @pl.loop(0, 2)
        def _(kk):
            for groups in GROUPS:
                def coef(form, i, r):
                    return cf[form, i, kk, r + HALO]

                def face_y(form, r, a, s_a, b, s_b):
                    return (coef(form, 4, r) * a + coef(form, 5, r) * s_a) + (
                        coef(form, 6, r) * b + coef(form, 7, r) * s_b
                    )

                start = []
                for g in groups:
                    q = [tile(src, g, kk, first + i) for i in (-2, -1, 0, 1)]
                    d = [q[i + 1] - q[i] for i in range(3)]
                    s = [minmod(d[0], d[1]), minmod(d[1], d[2])]
                    start.append((q[2], q[3], d[2], s[1], face_y(g // 4, first - 1, q[1], s[0], q[2], s[1])))

                unroll = count // ROUNDS

                def some(i, state):
                    base = first + unroll * i
                    ahead = [[tile(src, g, kk, base + j + 2) for g in groups] for j in range(unroll)]
                    results = []
                    for j in range(unroll):
                        r = base + j
                        after = []
                        for g, c_nn, (c, c_n, d_n, s, g_s) in zip(groups, ahead[j], state):
                            form = g // 4
                            d_nn = c_nn - c_n
                            s_n = minmod(d_nn, d_n)
                            g_n = face_y(form, r, c, s, c_n, s_n)
                            d_e = lanes(c, -1) - c
                            s_x = minmod(d_e, lanes(d_e, 1))
                            right = coef(form, 0, r) * c + coef(form, 1, r) * s_x
                            left = coef(form, 2, r) * c + coef(form, 3, r) * s_x
                            results.append(
                                c - ((right + lanes(left, -1)) - (lanes(right, 1) + left)) - (g_n - g_s)
                            )
                            after.append((c_n, c_nn, d_nn, s_n, g_n))
                        state = tuple(after)
                    for j in range(unroll):
                        for n, g in enumerate(groups):
                            put = pl.ds(pl.multiple_of(8 * (base + j + HALO), 8), 8)
                            dst[g, kk, put, :] = results[j * len(groups) + n]
                    return state

                lax.fori_loop(0, ROUNDS, some, tuple(start))

    def absorb(first, count):
        @pl.loop(0, count // 4)
        def _(i):
            for kk in range(2):
                results = []
                for j in range(4):
                    r = first + 4 * i + j
                    strip = tile(c2, 4, kk, r)
                    total = jnp.zeros((8, width), F32)
                    for g in range(4):
                        new = tile(c2, g, kk, r)
                        new = jnp.where(lane < 4, lanes(strip, -(32 * g + 8)), new)
                        new = jnp.where(lane >= width - 4, lanes(strip, width - 24 - 32 * g), new)
                        results.append(new)
                        total = total + uptakes[g] * jnp.abs(new)
                    results.append(jnp.sum(total, axis=0, keepdims=True))
                for j in range(4):
                    r = first + 4 * i + j
                    for g in range(4):
                        c2[g, kk, pl.ds(pl.multiple_of(8 * (r + HALO), 8), 8), :] = results[5 * j + g]
                    ab[kk, pl.ds(r, 1), :] = results[5 * j + 4]

    def layer(kk, first, count):
        dep = vs[1, 5, pl.ds(8 + first, count)]
        wet = wet_of((2 * t + kk).astype(F32), dep)
        return 0.25 * (0.2 + ab[kk, pl.ds(first, count)]) * wet, wet

    def send_layers(c):
        first, count = CHUNKS[c]
        s_own[c, 0:count] = layer(0, first, count)[0] + layer(1, first, count)[0]
        return [
            go(remote(s_own.at[c], s_got.at[c, d], s_s.at[c, d], s_r.at[c, d], {"trc": other[d]}))
            for d in range(3)
        ]

    def finish_chunk(c):
        first, count = CHUNKS[c]
        above = jnp.zeros((count, width), F32)
        for d in range(3):
            above = above + jnp.where(t - (d + 1) >= 0, 1.0, 0.0) * s_got[c, d, 0:count]
        light_in = surface[8 + first : 8 + first + count]
        part = pl.ds(first, count)
        for kk in range(2):
            lay, wet = layer(kk, first, count)
            over = light_in * jnp.exp(-above)
            o_t[kk, part] = th_in[kk, part] + over * (1.0 - jnp.exp(-lay))
            fl[kk, part] = DT * wet * (over / (over + 0.5))
            w01[kk, part] = DT * wet
            above = above + lay
        matrix = table[...]
        copies = []
        for n, (begin, size) in enumerate(PARTS[c]):

            @pl.loop(0, size // 4)
            def _(i):
                for kk in range(2):
                    r0 = begin + 4 * i
                    stacked = jnp.concatenate(
                        [jnp.concatenate([tile(c2, g, kk, r0 + j) for g in range(4)], axis=0) for j in range(4)],
                        axis=1,
                    )
                    mixed = jnp.dot(matrix, stacked, precision=lax.Precision.HIGHEST, preferred_element_type=F32)
                    results = []
                    for j in range(4):
                        light = fl[kk, pl.ds(r0 + j, 1), :]
                        wet = w01[kk, pl.ds(r0 + j, 1), :]
                        for g in range(4):
                            moved = stacked[8 * g : 8 * g + 8, width * j : width * (j + 1)]
                            mix = mixed[8 * g : 8 * g + 8, width * j : width * (j + 1)]
                            results.append(moved + wet * mix + light * (prod[g] * moved))
                    for j in range(4):
                        for g in range(4):
                            out[g, kk, pl.ds(pl.multiple_of(8 * (r0 + j), 8), 8), :] = results[4 * j + g]

            part8 = pl.ds(8 * begin, 8 * size)
            s = sum(len(p) for p in PARTS[:c]) + n
            copies.append([
                go(remote(out.at[other[d], :, part8], ry.at[t, :, part8], out_s.at[s, d], out_r.at[s, d], {"trc": other[d]}))
                for d in (1, 0, 2)
            ])
            here = pltpu.make_async_copy(out.at[t, :, part8], ry.at[t, :, part8], loc.at[s])
            here.start()
            copies[-1].append(here)
        return copies

    zero_tile = jnp.zeros((8, width), F32)
    done_pieces = 2
    layers = [None] * len(CHUNKS)
    results = [None] * len(CHUNKS)
    c1_done = -2
    stage_no = 0
    for c, (first, count) in enumerate(CHUNKS):
        for p in range(done_pieces, need[c]):
            for d in range(3):
                incoming[d, p].wait_recv()
            begin, size = pieces[p]
            if THROTTLE:
                send_pieces(p + 2)
            strips(begin, begin + size)
        done_pieces = need[c]
        end = first + count + 2
        if c == 0:
            lat[0].wait_recv()

            @pl.when(la == 0)
            def _():
                for g in range(5):
                    for kk in range(2):
                        for r in range(HALO):
                            c0[g, kk, 8 * r : 8 * r + 8] = zero_tile

        if c == len(CHUNKS) - 1:
            lat[1].wait_recv()

            @pl.when(la == n_lat - 1)
            def _():
                for g in range(5):
                    for kk in range(2):
                        for r in range(rows + HALO, rows + 2 * HALO):
                            c0[g, kk, 8 * r : 8 * r + 8] = zero_tile

        step(c0, c1, c1_done, end - c1_done)
        c1_done = end
        if c > 0:
            for copy in layers[c - 1]:
                copy.wait_recv()
            results[c - 1] = finish_chunk(c - 1)
        step(c1, c2, first, count)
        absorb(first, count)
        layers[c] = send_layers(c)

        if c == 0:
            stage.wait_recv()
            h1[1, own] = h_in[...] - (DT * 0.5) * (dp[1] + dp_got[1])
            edges = [
                go(remote(h1.at[1, own], h1.at[0, own], h_s.at[0], h_r.at[0], {"lon": east})),
                go(remote(h1.at[1, own], h1.at[2, own], h_s.at[1], h_r.at[1], {"lon": west})),
                go(remote(h1.at[1, top], h1.at[1, pl.ds(0, 8)], h_s.at[2], h_r.at[2], {"lat": north})),
                go(remote(h1.at[1, low], h1.at[1, pl.ds(rows + 8, 8)], h_s.at[3], h_r.at[3], {"lat": south})),
            ]

    for copy in edges:
        copy.wait_recv()

    @pl.when(la == 0)
    def _():
        h1[1, 0:8] = jnp.zeros((8, width), F32)

    @pl.when(la == n_lat - 1)
    def _():
        h1[1, rows + 8 : rows + 16] = jnp.zeros((8, width), F32)

    for b in (0, 2):
        h1[b, 0:8] = jnp.zeros((8, width), F32)
        h1[b, rows + 8 : rows + 16] = jnp.zeros((8, width), F32)
    wide_h = jnp.concatenate([h1[0], h1[1], h1[2]], axis=1)
    div = jnp.zeros((rows, width), F32)
    for kk in range(2):
        u, v = mom[kk], mom[2 + kk]
        div = div + divergence(u, v)
        new_u, new_v = momentum(u, v, wide_h, wet_of((2 * t + kk).astype(F32), wide_depth))
        o_u[kk] = new_u[8 : 8 + rows, width : 2 * width]
        o_v[kk] = new_v[8 : 8 + rows, width : 2 * width]
    dp[2] = div
    stage = dp_stage(2)
    for copy in layers[-1]:
        copy.wait_recv()
    results[-1] = finish_chunk(len(CHUNKS) - 1)

    stage.wait_recv()
    dp[3] = dp[2] + dp_got[2]
    stage = dp_stage(3)

    def unturn(src, first, count):
        for kk in range(2):
            fields = [ry[src, kk, pl.ds(8 * first + n, count, stride=8), :] for n in range(8)]
            for n in range(8):
                o_x[n, 2 * src + kk, pl.ds(first, count)] = fields[n]

    leaving = []

    def leave(near_ref, far_ref):
        leaving.append(pltpu.make_async_copy(near_ref, far_ref, away.at[len(leaving)]))
        leaving[-1].start()

    leave(o_u, far_u)
    leave(o_v, far_v)
    leave(o_t, far_t)
    unpacked, part_no = 0, 0
    for c in range(len(CHUNKS)):
        for n, (first, count) in enumerate(PARTS[c]):
            *copies, here = results[c][n]
            end = (first + count) // 8 * 8
            part = pl.ds(unpacked, end - unpacked)
            for copy, src in ((here, t), *((copies[i], source[d]) for i, d in enumerate((1, 0, 2)))):
                if copy is here:
                    copy.wait()
                else:
                    copy.wait_recv()
                if end > unpacked:
                    unturn(src, unpacked, end - unpacked)
                    leave(o_x.at[:, pl.ds(2 * src, 2), part], far_x.at[:, pl.ds(2 * src, 2), part])
            unpacked = end
            part_no += 1
            if part_no == N_PARTS - 1:
                stage.wait_recv()
                o_h[...] = h1[1, own] - (DT * 0.5) * (dp[3] + dp_got[3])
                leave(o_h, far_h)
    for copy in leaving:
        copy.wait()
    for copy in sends:
        copy.wait_send()


def place(*refs):
    far, to, near, come, leave = refs[:5], refs[5:10], refs[10:15], refs[15], refs[16]
    moves = []
    for i in range(5):
        parts = [slice(None)] if i else [pl.ds(2 * p, 2) for p in range(4)]
        for part in parts:
            n = len(moves)
            moves.append(
                (
                    pltpu.make_async_copy(far[i].at[part], near[i].at[part], come.at[n]),
                    pltpu.make_async_copy(near[i].at[part], to[i].at[part], leave.at[n]),
                )
            )
    for first, _ in moves:
        first.start()
    for first, second in moves:
        first.wait()
        second.start()
    for _, second in moves:
        second.wait()


def body(x, u, v, th, h, w, table, pace, uptake):
    tracers, levels, rows, width = x.shape
    smem = pl.BlockSpec(memory_space=pltpu.SMEM)
    ext = rows + 2 * HALO
    n_c = len(CHUNKS)
    n_p = len(in_pieces(rows)[0])
    most = -(-max(count for _, count in CHUNKS) // 8) * 8
    dma = lambda *s: pltpu.SemaphoreType.DMA(s)
    buf = lambda *s: pltpu.VMEM(s, F32)
    scratch = [
        *(pltpu.VMEM(a.shape, F32) for a in (x, u, u, u, h)),
        *(pltpu.VMEM(a.shape, a.dtype) for a in (x, u, v, th, h, w, table)),
        buf(4, 2, 8 * rows, width),
        buf(5, 2, 8 * ext, width),
        buf(5, 2, 8 * ext, width),
        buf(5, 2, 8 * ext, width),
        buf(4, 2, 8 * rows, width),
        buf(4, 2, 8 * rows, width),
        buf(2, 8, 8, width),
        buf(2, 8, 8, width),
        buf(2, 4, 2, 8, width),
        buf(2, 8, 2, rows + 16, width),
        buf(2, 8, 2, ext, 8, width),
        buf(3, 6, rows + 16, width),
        buf(2, rows, width),
        buf(2, rows, width),
        buf(4, rows + 16, 3 * width),
        buf(4, rows, width),
        buf(4, rows, width),
        buf(3, rows + 16, width),
        buf(2, rows, width),
        buf(n_c, most, width),
        buf(n_c, 3, most, width),
        buf(2, rows, width),
        buf(2, rows, width),
        buf(4, 8, width),
        pltpu.SemaphoreType.REGULAR,
        dma(3, n_p), dma(3, n_p),
        dma(2), dma(2),
        dma(3), dma(3),
        dma(2), dma(2),
        dma(4), dma(4),
        dma(4), dma(4),
        dma(4), dma(4),
        dma(n_c, 3), dma(n_c, 3),
        dma(N_PARTS, 3), dma(N_PARTS, 3),
        dma(N_PARTS + 2), dma(7), dma(4 + 4 * N_PARTS),
    ]
    field = jax.ShapeDtypeStruct(u.shape, F32)
    results = pl.pallas_call(
        kernel,
        out_shape=(
            jax.ShapeDtypeStruct(x.shape, F32), field, field, field, jax.ShapeDtypeStruct(h.shape, F32),
        ),
        in_specs=[pl.BlockSpec(memory_space=pltpu.HBM)] * 7 + [smem] * 2,
        out_specs=(pl.BlockSpec(memory_space=pltpu.HBM),) * 5,
        scratch_shapes=scratch,
        compiler_params=pltpu.CompilerParams(
            collective_id=0, has_side_effects=True, vmem_limit_bytes=62 * 1024 * 1024
        ),
    )(x, u, v, th, h, w, table, pace, uptake)

    return pl.pallas_call(
        place,
        out_shape=tuple(jax.ShapeDtypeStruct(r.shape, F32) for r in results),
        in_specs=[pl.BlockSpec(memory_space=pltpu.HBM)] * 5,
        out_specs=(pl.BlockSpec(memory_space=pltpu.HBM),) * 5,
        scratch_shapes=[*(pltpu.VMEM(r.shape, F32) for r in results), dma(8), dma(8)],
        compiler_params=pltpu.CompilerParams(vmem_limit_bytes=62 * 1024 * 1024),
    )(*results)


def solution(mesh):
    return jax.shard_map(
        body,
        mesh=mesh,
        in_specs=(
            P("trc", None, "lat", "lon"),
            P("trc", "lat", "lon"),
            P("trc", "lat", "lon"),
            P("trc", "lat", "lon"),
            P("lat", "lon"),
            P("lat", "lon"),
            P(),
            P(),
            P(),
        ),
        out_specs=(
            P("trc", None, "lat", "lon"),
            P("trc", "lat", "lon"),
            P("trc", "lat", "lon"),
            P("trc", "lat", "lon"),
            P("lat", "lon"),
        ),
        check_vma=False,
    )
```

```python
import functools
import math

import jax
import jax.numpy as jnp
from jax import lax
from jax.experimental import pallas as pl
from jax.experimental.pallas import tpu as pltpu
from jax.sharding import PartitionSpec as P

MESH = pl.DeviceIdType.MESH
F32 = jnp.float32
DT = 0.1
CHUNKS = ((0, 12), (12, 20))
PARTS = (((0, 12),), ((12, 8), (20, 12)))
N_PARTS = sum(len(p) for p in PARTS)
HALO = 4
THROTTLE = True
ROUNDS = 2
GROUPS = ((0, 1, 2, 3, 4),)


def in_pieces(rows):
    pieces = [(0, HALO), (rows - HALO, HALO)]
    need, done = [], HALO
    for first, count in CHUNKS:
        end = min(first + count + HALO, rows - HALO)
        if end > done:
            pieces.append((done, end - done))
            done = end
        need.append(len(pieces))
    return pieces, need


def minmod(x, y):
    return jnp.maximum(jnp.minimum(x, y), jnp.minimum(jnp.maximum(x, y), 0.0))


def lanes(x, shift):
    shift = shift % x.shape[-1]
    return pltpu.roll(x, shift, x.ndim - 1) if shift else x


def rows_by(x, shift):
    shift = -shift % x.shape[0]
    return pltpu.roll(x, shift, 0) if shift else x


def kernel(
    x_far, u_far, v_far, th_far, h_far, w_far, table_far, pace, uptake,
    far_x, far_u, far_v, far_t, far_h,
    o_x, o_u, o_v, o_t, o_h,
    x, u_in, v_in, th_in, h_in, w_in, table,
    tx, c0, c1, c2, out, ry, pk_own, pk_got, sk, cc, cf,
    vs, ve_own, ve_got, mom, dp, dp_got, h1, ab, s_own, s_got, fl, w01, prod,
    ready, in_s, in_r, lon_s, lon_r, sk_s, sk_r, lat_s, lat_r, vs_s, vs_r, dp_s, dp_r, h_s, h_r,
    s_s, s_r, out_s, out_r, loc, near, away,
):
    rows, width = h_in.shape
    n_lat, n_lon = lax.axis_size("lat"), lax.axis_size("lon")
    t, la, lo = lax.axis_index("trc"), lax.axis_index("lat"), lax.axis_index("lon")
    other = [lax.rem(t + d, 4) for d in (1, 2, 3)]
    source = [lax.rem(t + 4 - d, 4) for d in (1, 2, 3)]
    east, west = lax.rem(lo + 1, n_lon), lax.rem(lo + n_lon - 1, n_lon)
    north, south = lax.rem(la + 1, n_lat), lax.rem(la + n_lat - 1, n_lat)
    pieces, need = in_pieces(rows)

    def remote(src, dst, send, recv, where):
        return pltpu.make_async_remote_copy(
            src_ref=src, dst_ref=dst, send_sem=send, recv_sem=recv, device_id=where, device_id_type=MESH
        )

    sends = []

    def go(copy):
        copy.start()
        sends.append(copy)
        return copy

    barrier = pltpu.get_barrier_semaphore()
    friends = [{"trc": g} for g in other] + [{"lon": west}, {"lat": north}, {"lat": south}]
    for friend in friends:
        pl.semaphore_signal(barrier, inc=1, device_id=friend, device_id_type=MESH)

    fetched = []
    for i, (far, close) in enumerate(
        ((u_far, u_in), (v_far, v_in), (h_far, h_in), (w_far, w_in), (x_far, x), (th_far, th_in), (table_far, table))
    ):
        fetched.append(pltpu.make_async_copy(far, close, near.at[i]))
        fetched[-1].start()
    for copy in fetched[:4]:
        copy.wait()

    depth = w_in[...].astype(F32)

    def wet_of(level, depths):
        return jnp.where(level < depths, 1.0, 0.0)

    own = pl.ds(8, rows)
    for kk in range(2):
        wet = wet_of((2 * t + kk).astype(F32), depth)
        vs[1, kk, own] = wet * u_in[kk]
        vs[1, 2 + kk, own] = wet * v_in[kk]
    vs[1, 4, own] = h_in[...]
    vs[1, 5, own] = depth

    lane = lax.broadcasted_iota(jnp.int32, (8, width), 1)
    slot = lane // 8
    lane32 = lane % 32
    slot4 = lane // 4
    fetched[4].wait()

    @pl.loop(0, 4)
    def _(target):
        for kk in range(2):
            fields = [x[n, 2 * target + kk] for n in range(8)]
            for n in range(8):
                tx[target, kk, pl.ds(n, rows, stride=8), :] = fields[n]

    @pl.loop(0, 4)
    def _(target):
        for kk in range(2):
            to_west = to_east = jnp.zeros((8, width), F32)
            for j in range(rows):
                turned = lanes(tx[target, kk, pl.ds(8 * j, 8), :], 4 * (j + 1))
                to_west = jnp.where(slot4 == (j + 1) % 32, turned, to_west)
                to_east = jnp.where(slot4 == j, turned, to_east)
            pk_own[0, 2 * target + kk] = to_west
            pk_own[1, 2 * target + kk] = to_east

    lane_v = lax.broadcasted_iota(jnp.int32, (rows, width), 1) // 8
    to_west = to_east = jnp.zeros((rows, width), F32)
    for f in range(6):
        field = vs[1, f, own]
        to_west = jnp.where(lane_v == f, lanes(field, 8 * f), to_west)
        to_east = jnp.where(lane_v == f, lanes(field, 8 * f + 8), to_east)
    ve_own[0], ve_own[1] = to_west, to_east

    mine = pltpu.make_async_copy(tx.at[t], c0.at[t, :, pl.ds(8 * HALO, 8 * rows)], loc.at[N_PARTS])
    mine.start()
    fetched[5].wait()
    fetched[6].wait()
    pl.semaphore_wait(barrier, len(friends))
    pl.semaphore_signal(ready, inc=1, device_id={"lon": east}, device_id_type=MESH)
    vs_lon = [
        go(remote(ve_own.at[1], ve_got.at[1], vs_s.at[0], vs_r.at[0], {"lon": east})),
    ]
    pk = [go(remote(pk_own.at[1], pk_got.at[1], lon_s.at[0], lon_r.at[0], {"lon": east}))]
    incoming = {}

    def send_piece(d, p):
        first, count = pieces[p]
        incoming[d, p] = go(
            remote(
                tx.at[other[d], :, pl.ds(8 * first, 8 * count)],
                c0.at[t, :, pl.ds(8 * (first + HALO), 8 * count)],
                in_s.at[d, p], in_r.at[d, p], {"trc": other[d]},
            )
        )

    def send_pieces(p):
        if p < len(pieces):
            for d in (1, 0, 2):
                send_piece(d, p)

    send_pieces(0)
    send_pieces(1)
    send_pieces(2)
    if not THROTTLE:
        for p in range(3, len(pieces)):
            send_pieces(p)

    pl.semaphore_wait(ready, 1)
    vs_lon.append(go(remote(ve_own.at[0], ve_got.at[0], vs_s.at[1], vs_r.at[1], {"lon": west})))
    pk.append(go(remote(pk_own.at[0], pk_got.at[0], lon_s.at[1], lon_r.at[1], {"lon": west})))
    for copy in vs_lon:
        copy.wait_recv()
    for f in range(6):
        vs[0, f, own] = lanes(ve_got[1], width - 8 - 8 * f)
        vs[2, f, own] = lanes(ve_got[0], -8 * f)
    top, low = pl.ds(rows, 8), pl.ds(8, 8)
    vs_lat = [
        go(remote(vs.at[:, :, top], vs.at[:, :, pl.ds(0, 8)], vs_s.at[2], vs_r.at[2], {"lat": north})),
        go(remote(vs.at[:, :, low], vs.at[:, :, pl.ds(rows + 8, 8)], vs_s.at[3], vs_r.at[3], {"lat": south})),
    ]

    for copy in pk:
        copy.wait_recv()
    strip_in = [
        go(remote(pk_got.at[:, pl.ds(2 * other[d], 2)], sk.at[:, t], sk_s.at[d], sk_r.at[d], {"trc": other[d]}))
        for d in range(3)
    ]
    mine_too = pltpu.make_async_copy(pk_got.at[:, pl.ds(2 * t, 2)], sk.at[:, t], loc.at[N_PARTS + 1])
    mine_too.start()

    def tile(buf, g, kk, r):
        return buf[g, kk, pl.ds(pl.multiple_of(8 * (r + HALO), 8), 8), :]

    def strips(begin, end):
        @pl.loop(0, (end - begin) // 4)
        def _(quad):
            results = []
            for i in range(4):
                r = begin + 4 * quad + i
                for kk in range(2):
                    strip = jnp.zeros((8, width), F32)
                    for g in range(4):
                        here = tile(c0, g, kk, r)
                        parts = (
                            pltpu.roll(sk[1, g, kk], (32 * g + 4 + width - 4 * r) % width, 1),
                            lanes(here, 32 * g + 8),
                            lanes(here, 32 * g + 24),
                            pltpu.roll(sk[0, g, kk], (32 * g + 20 + width - 4 * r) % width, 1),
                        )
                        for n, part in enumerate(parts):
                            strip = jnp.where(slot == 4 * g + n, part, strip)
                    results.append(strip)
            for i in range(4):
                for kk in range(2):
                    put = pl.ds(pl.multiple_of(8 * (begin + 4 * quad + i + HALO), 8), 8)
                    c0[4, kk, put, :] = results[2 * i + kk]

    for p in (0, 1):
        for d in range(3):
            incoming[d, p].wait_recv()
    if THROTTLE:
        send_pieces(3)
    mine.wait()
    mine_too.wait()
    for copy in strip_in:
        copy.wait_recv()
    strips(0, HALO)
    strips(rows - HALO, rows)
    lat = [
        go(remote(c0.at[:, :, pl.ds(8 * rows, 8 * HALO)], c0.at[:, :, pl.ds(0, 8 * HALO)],
                  lat_s.at[0], lat_r.at[0], {"lat": north})),
        go(remote(c0.at[:, :, pl.ds(8 * HALO, 8 * HALO)], c0.at[:, :, pl.ds(8 * (rows + HALO), 8 * HALO)],
                  lat_s.at[1], lat_r.at[1], {"lat": south})),
    ]
    for copy in vs_lat:
        copy.wait_recv()

    @pl.when(la == 0)
    def _():
        for b in range(3):
            for f in range(6):
                vs[b, f, 0:8] = jnp.zeros((8, width), F32)

    @pl.when(la == n_lat - 1)
    def _():
        for b in range(3):
            for f in range(6):
                vs[b, f, rows + 8 : rows + 16] = jnp.zeros((8, width), F32)

    vlane = lax.broadcasted_iota(jnp.int32, (rows + 16, width), 1) % 32

    def strip_form(f):
        w_, o_, e_ = vs[0, f], vs[1, f], vs[2, f]
        left = jnp.where(vlane < 8, lanes(w_, 8), lanes(o_, 8))
        right = jnp.where(vlane < 24, lanes(o_, 24), lanes(e_, 24))
        first = jnp.where(vlane < 16, left, right)
        lane_ = lax.broadcasted_iota(jnp.int32, first.shape, 1)
        first = jnp.where(lane_ < 32, first, 0.0)
        first = first + lanes(first, 32)
        return first + lanes(first, 64)

    def weights(a):
        ap, an = jnp.maximum(a, 0.0), jnp.minimum(a, 0.0)
        return ap, 0.5 * ap * (1.0 - ap), an, -0.5 * an * (1.0 + an)

    for form in range(2):
        get = (lambda f: vs[1, f]) if form == 0 else strip_form
        dep = get(5)
        for kk in range(2):
            wet = wet_of((2 * t + kk).astype(F32), dep)
            u, v = get(kk), get(2 + kk)
            ax = 0.5 * (u + lanes(u, -1)) * wet * lanes(wet, -1)
            ap, bp, an, bn = weights(ax)
            cc[form, 0, kk], cc[form, 1, kk] = ap, bp
            cc[form, 2, kk], cc[form, 3, kk] = lanes(an, 1), lanes(bn, 1)
            ay = 0.5 * (v + rows_by(v, 1)) * wet * rows_by(wet, 1)
            for i, w in enumerate(weights(ay)):
                cc[form, 4 + i, kk] = w

    @pl.loop(0, (rows + 2 * HALO - 1) // 3)
    def _(three):
        every = [
            (form, i, kk, 1 + 3 * three + n)
            for n in range(3) for form in range(2) for i in range(8) for kk in range(2)
        ]
        wide_rows = [jnp.broadcast_to(cc[f, i, kk, pl.ds(r + 8 - HALO, 1), :], (8, width)) for f, i, kk, r in every]
        for (f, i, kk, r), value in zip(every, wide_rows):
            cf[f, i, kk, r] = value

    big = rows + 16
    row_no = (la * rows - 8 + lax.broadcasted_iota(jnp.int32, (big, 1), 0)).astype(F32)
    angle = math.pi * ((row_no + 0.5) / (rows * n_lat) - 0.5)
    coriolis = 0.5 * jnp.sin(angle)
    surface = 1.0 + jnp.cos(angle)
    wide = lambda ref, f: jnp.concatenate([ref[0, f], ref[1, f], ref[2, f]], axis=1)

    def momentum(u, v, h, wet):
        h_x = 0.5 * (lanes(h, -1) - lanes(h, 1))
        h_y = 0.5 * (rows_by(h, 1) - rows_by(h, -1))
        lap_u = rows_by(u, 1) + rows_by(u, -1) + lanes(u, -1) + lanes(u, 1) - 4.0 * u
        lap_v = rows_by(v, 1) + rows_by(v, -1) + lanes(v, -1) + lanes(v, 1) - 4.0 * v
        new_u = wet * (u + DT * (coriolis * v - h_x + 0.2 * lap_u - 0.05 * u))
        new_v = wet * (v + DT * (-coriolis * u - h_y + 0.2 * lap_v - 0.05 * v))
        return new_u, new_v

    def divergence(u, v):
        d = 0.5 * (lanes(u, -1) - lanes(u, 1)) + 0.5 * (rows_by(v, 1) - rows_by(v, -1))
        return d[8 : 8 + rows, width : 2 * width]

    def dp_stage(i):
        partner = t + 1 - 2 * lax.rem(t, 2) if i % 2 == 0 else 3 - t
        return go(remote(dp.at[i], dp_got.at[i], dp_s.at[i], dp_r.at[i], {"trc": partner}))

    wide_depth = wide(vs, 5)
    wide_h = wide(vs, 4)
    div = jnp.zeros((rows, width), F32)
    for kk in range(2):
        u, v = wide(vs, kk), wide(vs, 2 + kk)
        div = div + divergence(u, v)
        mom[kk], mom[2 + kk] = momentum(u, v, wide_h, wet_of((2 * t + kk).astype(F32), wide_depth))
    dp[0] = div
    stage = dp_stage(0)

    stage.wait_recv()
    dp[1] = dp[0] + dp_got[0]
    stage = dp_stage(1)

    sub = lax.broadcasted_iota(jnp.int32, (8, width), 0)

    def column(ref, g):
        col = jnp.full((8, width), ref[8 * g], F32)
        for n in range(1, 8):
            col = jnp.where(sub == n, ref[8 * g + n], col)
        return col

    uptakes = [column(uptake, g) for g in range(4)]
    for g in range(4):
        prod[g] = column(pace, g)

    def step(src, dst, first, count):
        @pl.loop(0, 2)
        def _(kk):
            for groups in GROUPS:
                def coef(form, i, r):
                    return cf[form, i, kk, r + HALO]

                def face_y(form, r, a, s_a, b, s_b):
                    return (coef(form, 4, r) * a + coef(form, 5, r) * s_a) + (
                        coef(form, 6, r) * b + coef(form, 7, r) * s_b
                    )

                start = []
                for g in groups:
                    q = [tile(src, g, kk, first + i) for i in (-2, -1, 0, 1)]
                    d = [q[i + 1] - q[i] for i in range(3)]
                    s = [minmod(d[0], d[1]), minmod(d[1], d[2])]
                    start.append((q[2], q[3], d[2], s[1], face_y(g // 4, first - 1, q[1], s[0], q[2], s[1])))

                unroll = count // ROUNDS

                def some(i, state):
                    base = first + unroll * i
                    ahead = [[tile(src, g, kk, base + j + 2) for g in groups] for j in range(unroll)]
                    results = []
                    for j in range(unroll):
                        r = base + j
                        after = []
                        for g, c_nn, (c, c_n, d_n, s, g_s) in zip(groups, ahead[j], state):
                            form = g // 4
                            d_nn = c_nn - c_n
                            s_n = minmod(d_nn, d_n)
                            g_n = face_y(form, r, c, s, c_n, s_n)
                            d_e = lanes(c, -1) - c
                            s_x = minmod(d_e, lanes(d_e, 1))
                            right = coef(form, 0, r) * c + coef(form, 1, r) * s_x
                            left = coef(form, 2, r) * c + coef(form, 3, r) * s_x
                            results.append(
                                c - ((right + lanes(left, -1)) - (lanes(right, 1) + left)) - (g_n - g_s)
                            )
                            after.append((c_n, c_nn, d_nn, s_n, g_n))
                        state = tuple(after)
                    for j in range(unroll):
                        for n, g in enumerate(groups):
                            put = pl.ds(pl.multiple_of(8 * (base + j + HALO), 8), 8)
                            dst[g, kk, put, :] = results[j * len(groups) + n]
                    return state

                lax.fori_loop(0, ROUNDS, some, tuple(start))

    def absorb(first, count):
        @pl.loop(0, count // 4)
        def _(i):
            for kk in range(2):
                results = []
                for j in range(4):
                    r = first + 4 * i + j
                    strip = tile(c2, 4, kk, r)
                    total = jnp.zeros((8, width), F32)
                    for g in range(4):
                        new = tile(c2, g, kk, r)
                        new = jnp.where(lane < 4, lanes(strip, -(32 * g + 8)), new)
                        new = jnp.where(lane >= width - 4, lanes(strip, width - 24 - 32 * g), new)
                        results.append(new)
                        total = total + uptakes[g] * jnp.abs(new)
                    results.append(jnp.sum(total, axis=0, keepdims=True))
                for j in range(4):
                    r = first + 4 * i + j
                    for g in range(4):
                        c2[g, kk, pl.ds(pl.multiple_of(8 * (r + HALO), 8), 8), :] = results[5 * j + g]
                    ab[kk, pl.ds(r, 1), :] = results[5 * j + 4]

    def layer(kk, first, count):
        dep = vs[1, 5, pl.ds(8 + first, count)]
        wet = wet_of((2 * t + kk).astype(F32), dep)
        return 0.25 * (0.2 + ab[kk, pl.ds(first, count)]) * wet, wet

    def send_layers(c):
        first, count = CHUNKS[c]
        s_own[c, 0:count] = layer(0, first, count)[0] + layer(1, first, count)[0]
        return [
            go(remote(s_own.at[c], s_got.at[c, d], s_s.at[c, d], s_r.at[c, d], {"trc": other[d]}))
            for d in range(3)
        ]

    def finish_chunk(c):
        first, count = CHUNKS[c]
        above = jnp.zeros((count, width), F32)
        for d in range(3):
            above = above + jnp.where(t - (d + 1) >= 0, 1.0, 0.0) * s_got[c, d, 0:count]
        light_in = surface[8 + first : 8 + first + count]
        part = pl.ds(first, count)
        for kk in range(2):
            lay, wet = layer(kk, first, count)
            over = light_in * jnp.exp(-above)
            o_t[kk, part] = th_in[kk, part] + over * (1.0 - jnp.exp(-lay))
            fl[kk, part] = DT * wet * (over / (over + 0.5))
            w01[kk, part] = DT * wet
            above = above + lay
        matrix = table[...]
        copies = []
        for n, (begin, size) in enumerate(PARTS[c]):

            @pl.loop(0, size // 4)
            def _(i):
                for kk in range(2):
                    r0 = begin + 4 * i
                    stacked = jnp.concatenate(
                        [jnp.concatenate([tile(c2, g, kk, r0 + j) for g in range(4)], axis=0) for j in range(4)],
                        axis=1,
                    )
                    mixed = jnp.dot(matrix, stacked, precision=lax.Precision.HIGHEST, preferred_element_type=F32)
                    results = []
                    for j in range(4):
                        light = fl[kk, pl.ds(r0 + j, 1), :]
                        wet = w01[kk, pl.ds(r0 + j, 1), :]
                        for g in range(4):
                            moved = stacked[8 * g : 8 * g + 8, width * j : width * (j + 1)]
                            mix = mixed[8 * g : 8 * g + 8, width * j : width * (j + 1)]
                            results.append(moved + wet * mix + light * (prod[g] * moved))
                    for j in range(4):
                        for g in range(4):
                            out[g, kk, pl.ds(pl.multiple_of(8 * (r0 + j), 8), 8), :] = results[4 * j + g]

            part8 = pl.ds(8 * begin, 8 * size)
            s = sum(len(p) for p in PARTS[:c]) + n
            copies.append([
                go(remote(out.at[other[d], :, part8], ry.at[t, :, part8], out_s.at[s, d], out_r.at[s, d], {"trc": other[d]}))
                for d in (1, 0, 2)
            ])
            here = pltpu.make_async_copy(out.at[t, :, part8], ry.at[t, :, part8], loc.at[s])
            here.start()
            copies[-1].append(here)
        return copies

    zero_tile = jnp.zeros((8, width), F32)
    done_pieces = 2
    layers = [None] * len(CHUNKS)
    results = [None] * len(CHUNKS)
    c1_done = -2
    stage_no = 0
    for c, (first, count) in enumerate(CHUNKS):
        for p in range(done_pieces, need[c]):
            for d in range(3):
                incoming[d, p].wait_recv()
            begin, size = pieces[p]
            if THROTTLE:
                send_pieces(p + 2)
            strips(begin, begin + size)
        done_pieces = need[c]
        end = first + count + 2
        if c == 0:
            lat[0].wait_recv()

            @pl.when(la == 0)
            def _():
                for g in range(5):
                    for kk in range(2):
                        for r in range(HALO):
                            c0[g, kk, 8 * r : 8 * r + 8] = zero_tile

        if c == len(CHUNKS) - 1:
            lat[1].wait_recv()

            @pl.when(la == n_lat - 1)
            def _():
                for g in range(5):
                    for kk in range(2):
                        for r in range(rows + HALO, rows + 2 * HALO):
                            c0[g, kk, 8 * r : 8 * r + 8] = zero_tile

        step(c0, c1, c1_done, end - c1_done)
        c1_done = end
        if c > 0:
            for copy in layers[c - 1]:
                copy.wait_recv()
            results[c - 1] = finish_chunk(c - 1)
        step(c1, c2, first, count)
        absorb(first, count)
        layers[c] = send_layers(c)

        if c == 0:
            stage.wait_recv()
            h1[1, own] = h_in[...] - (DT * 0.5) * (dp[1] + dp_got[1])
            edges = [
                go(remote(h1.at[1, own], h1.at[0, own], h_s.at[0], h_r.at[0], {"lon": east})),
                go(remote(h1.at[1, own], h1.at[2, own], h_s.at[1], h_r.at[1], {"lon": west})),
                go(remote(h1.at[1, top], h1.at[1, pl.ds(0, 8)], h_s.at[2], h_r.at[2], {"lat": north})),
                go(remote(h1.at[1, low], h1.at[1, pl.ds(rows + 8, 8)], h_s.at[3], h_r.at[3], {"lat": south})),
            ]

    for copy in edges:
        copy.wait_recv()

    @pl.when(la == 0)
    def _():
        h1[1, 0:8] = jnp.zeros((8, width), F32)

    @pl.when(la == n_lat - 1)
    def _():
        h1[1, rows + 8 : rows + 16] = jnp.zeros((8, width), F32)

    for b in (0, 2):
        h1[b, 0:8] = jnp.zeros((8, width), F32)
        h1[b, rows + 8 : rows + 16] = jnp.zeros((8, width), F32)
    wide_h = jnp.concatenate([h1[0], h1[1], h1[2]], axis=1)
    div = jnp.zeros((rows, width), F32)
    for kk in range(2):
        u, v = mom[kk], mom[2 + kk]
        div = div + divergence(u, v)
        new_u, new_v = momentum(u, v, wide_h, wet_of((2 * t + kk).astype(F32), wide_depth))
        o_u[kk] = new_u[8 : 8 + rows, width : 2 * width]
        o_v[kk] = new_v[8 : 8 + rows, width : 2 * width]
    dp[2] = div
    stage = dp_stage(2)
    for copy in layers[-1]:
        copy.wait_recv()
    results[-1] = finish_chunk(len(CHUNKS) - 1)

    stage.wait_recv()
    dp[3] = dp[2] + dp_got[2]
    stage = dp_stage(3)

    def unturn(src, first, count):
        for kk in range(2):
            fields = [ry[src, kk, pl.ds(8 * first + n, count, stride=8), :] for n in range(8)]
            for n in range(8):
                o_x[n, 2 * src + kk, pl.ds(first, count)] = fields[n]

    leaving = []

    def leave(near_ref, far_ref):
        leaving.append(pltpu.make_async_copy(near_ref, far_ref, away.at[len(leaving)]))
        leaving[-1].start()

    leave(o_u, far_u)
    leave(o_v, far_v)
    leave(o_t, far_t)
    unpacked, part_no = 0, 0
    for c in range(len(CHUNKS)):
        for n, (first, count) in enumerate(PARTS[c]):
            *copies, here = results[c][n]
            end = (first + count) // 8 * 8
            part = pl.ds(unpacked, end - unpacked)
            for copy, src in ((here, t), *((copies[i], source[d]) for i, d in enumerate((1, 0, 2)))):
                if copy is here:
                    copy.wait()
                else:
                    copy.wait_recv()
                if end > unpacked:
                    unturn(src, unpacked, end - unpacked)
                    leave(o_x.at[:, pl.ds(2 * src, 2), part], far_x.at[:, pl.ds(2 * src, 2), part])
            unpacked = end
            part_no += 1
            if part_no == N_PARTS - 1:
                stage.wait_recv()
                o_h[...] = h1[1, own] - (DT * 0.5) * (dp[3] + dp_got[3])
                leave(o_h, far_h)
    for copy in leaving:
        copy.wait()
    for copy in sends:
        copy.wait_send()


def place(*refs):
    far, to, near, come, leave = refs[:5], refs[5:10], refs[10:15], refs[15], refs[16]
    moves = []
    for i in range(5):
        parts = [slice(None)] if i else [pl.ds(2 * p, 2) for p in range(4)]
        for part in parts:
            n = len(moves)
            moves.append(
                (
                    pltpu.make_async_copy(far[i].at[part], near[i].at[part], come.at[n]),
                    pltpu.make_async_copy(near[i].at[part], to[i].at[part], leave.at[n]),
                )
            )
    for first, _ in moves:
        first.start()
    for first, second in moves:
        first.wait()
        second.start()
    for _, second in moves:
        second.wait()


def body(x, u, v, th, h, w, table, pace, uptake):
    tracers, levels, rows, width = x.shape
    smem = pl.BlockSpec(memory_space=pltpu.SMEM)
    ext = rows + 2 * HALO
    n_c = len(CHUNKS)
    n_p = len(in_pieces(rows)[0])
    most = -(-max(count for _, count in CHUNKS) // 8) * 8
    dma = lambda *s: pltpu.SemaphoreType.DMA(s)
    buf = lambda *s: pltpu.VMEM(s, F32)
    scratch = [
        *(pltpu.VMEM(a.shape, F32) for a in (x, u, u, u, h)),
        *(pltpu.VMEM(a.shape, a.dtype) for a in (x, u, v, th, h, w, table)),
        buf(4, 2, 8 * rows, width),
        buf(5, 2, 8 * ext, width),
        buf(5, 2, 8 * ext, width),
        buf(5, 2, 8 * ext, width),
        buf(4, 2, 8 * rows, width),
        buf(4, 2, 8 * rows, width),
        buf(2, 8, 8, width),
        buf(2, 8, 8, width),
        buf(2, 4, 2, 8, width),
        buf(2, 8, 2, rows + 16, width),
        buf(2, 8, 2, ext, 8, width),
        buf(3, 6, rows + 16, width),
        buf(2, rows, width),
        buf(2, rows, width),
        buf(4, rows + 16, 3 * width),
        buf(4, rows, width),
        buf(4, rows, width),
        buf(3, rows + 16, width),
        buf(2, rows, width),
        buf(n_c, most, width),
        buf(n_c, 3, most, width),
        buf(2, rows, width),
        buf(2, rows, width),
        buf(4, 8, width),
        pltpu.SemaphoreType.REGULAR,
        dma(3, n_p), dma(3, n_p),
        dma(2), dma(2),
        dma(3), dma(3),
        dma(2), dma(2),
        dma(4), dma(4),
        dma(4), dma(4),
        dma(4), dma(4),
        dma(n_c, 3), dma(n_c, 3),
        dma(N_PARTS, 3), dma(N_PARTS, 3),
        dma(N_PARTS + 2), dma(7), dma(4 + 4 * N_PARTS),
    ]
    field = jax.ShapeDtypeStruct(u.shape, F32)
    results = pl.pallas_call(
        kernel,
        out_shape=(
            jax.ShapeDtypeStruct(x.shape, F32), field, field, field, jax.ShapeDtypeStruct(h.shape, F32),
        ),
        in_specs=[pl.BlockSpec(memory_space=pltpu.HBM)] * 7 + [smem] * 2,
        out_specs=(pl.BlockSpec(memory_space=pltpu.HBM),) * 5,
        scratch_shapes=scratch,
        compiler_params=pltpu.CompilerParams(
            collective_id=0, has_side_effects=True, vmem_limit_bytes=62 * 1024 * 1024
        ),
    )(x, u, v, th, h, w, table, pace, uptake)

    return pl.pallas_call(
        place,
        out_shape=tuple(jax.ShapeDtypeStruct(r.shape, F32) for r in results),
        in_specs=[pl.BlockSpec(memory_space=pltpu.HBM)] * 5,
        out_specs=(pl.BlockSpec(memory_space=pltpu.HBM),) * 5,
        scratch_shapes=[*(pltpu.VMEM(r.shape, F32) for r in results), dma(8), dma(8)],
        compiler_params=pltpu.CompilerParams(vmem_limit_bytes=62 * 1024 * 1024),
    )(*results)


def solution(mesh):
    return jax.shard_map(
        body,
        mesh=mesh,
        in_specs=(
            P("trc", None, "lat", "lon"),
            P("trc", "lat", "lon"),
            P("trc", "lat", "lon"),
            P("trc", "lat", "lon"),
            P("lat", "lon"),
            P("lat", "lon"),
            P(),
            P(),
            P(),
        ),
        out_specs=(
            P("trc", None, "lat", "lon"),
            P("trc", "lat", "lon"),
            P("trc", "lat", "lon"),
            P("trc", "lat", "lon"),
            P("lat", "lon"),
        ),
        check_vma=False,
    )
```
